32 devices in a mesh: ctx: 8 (over y, x, core), fsdp: 4 (over z).
Axes of the slice: x: 2, y: 2, z: 4, core: 2. Of those that a mesh axis runs over, the one named last changes fastest.
Arguments:
- layer_in: bfloat16 [4, 2048, 2048], P('fsdp', 'ctx'), may hold values from -6 to 6
- cotangent: bfloat16 [4, 2048, 2048], P('fsdp', 'ctx'), may hold values from -6 to 6
- block_map: int32 [4, 8], P('fsdp'), may hold values from 0 to 7, as said below
- attn_in: float32 [2048, 6144], P(('ctx', 'fsdp')), may hold values from -0.125 to 0.125
- attn_out: float32 [2048, 2048], P(('ctx', 'fsdp')), may hold values from -1 to 1
- ffn_in: float32 [2048, 11264], P(('ctx', 'fsdp')), may hold values from -0.125 to 0.125
- ffn_out: float32 [5632, 2048], P(('ctx', 'fsdp')), may hold values from -0.15625 to 0.15625
- vectors: float32 [2048, 7], P(('ctx', 'fsdp')), may hold values from -2.5 to 3.5
- first_attn_in: float32 [2048, 6144], P(('ctx', 'fsdp')), may hold values from -9.1552734e-05 to 9.1552734e-05
- first_attn_out: float32 [2048, 2048], P(('ctx', 'fsdp')), may hold values from -9.1552734e-05 to 9.1552734e-05
- first_ffn_in: float32 [2048, 11264], P(('ctx', 'fsdp')), may hold values from -9.1552734e-05 to 9.1552734e-05
- first_ffn_out: float32 [5632, 2048], P(('ctx', 'fsdp')), may hold values from -9.1552734e-05 to 9.1552734e-05
- first_vectors: float32 [2048, 7], P(('ctx', 'fsdp')), may hold values from -9.1552734e-05 to 9.1552734e-05
- second_attn_in: float32 [2048, 6144], P(('ctx', 'fsdp')), may hold values from 9.728656e-10 to 3.8914623e-09
- second_attn_out: float32 [2048, 2048], P(('ctx', 'fsdp')), may hold values from 9.728656e-10 to 3.8914623e-09
- second_ffn_in: float32 [2048, 11264], P(('ctx', 'fsdp')), may hold values from 9.728656e-10 to 3.8914623e-09
- second_ffn_out: float32 [5632, 2048], P(('ctx', 'fsdp')), may hold values from 9.728656e-10 to 3.8914623e-09
- second_vectors: float32 [2048, 7], P(('ctx', 'fsdp')), may hold values from 9.728656e-10 to 3.8914623e-09
Outputs:
- layer_out: bfloat16 [4, 2048, 2048], P('fsdp', 'ctx')
- input_grad: float32 [4, 2048, 2048], P('fsdp', 'ctx')
- grad_norm: float32 [], replicated
- new_attn_in: float32 [2048, 6144], P(('ctx', 'fsdp'))
- new_first_attn_in: float32 [2048, 6144], P(('ctx', 'fsdp'))
- new_second_attn_in: float32 [2048, 6144], P(('ctx', 'fsdp'))
- new_attn_out: float32 [2048, 2048], P(('ctx', 'fsdp'))
- new_first_attn_out: float32 [2048, 2048], P(('ctx', 'fsdp'))
- new_second_attn_out: float32 [2048, 2048], P(('ctx', 'fsdp'))
- new_ffn_in: float32 [2048, 11264], P(('ctx', 'fsdp'))
- new_first_ffn_in: float32 [2048, 11264], P(('ctx', 'fsdp'))
- new_second_ffn_in: float32 [2048, 11264], P(('ctx', 'fsdp'))
- new_ffn_out: float32 [5632, 2048], P(('ctx', 'fsdp'))
- new_first_ffn_out: float32 [5632, 2048], P(('ctx', 'fsdp'))
- new_second_ffn_out: float32 [5632, 2048], P(('ctx', 'fsdp'))
- new_vectors: float32 [2048, 7], P(('ctx', 'fsdp'))
- new_first_vectors: float32 [2048, 7], P(('ctx', 'fsdp'))
- new_second_vectors: float32 [2048, 7], P(('ctx', 'fsdp'))
The draws below stay inside these ranges and needn't reach their ends.
Inputs may be any that keep to these rules, and one draw needn't show every extreme that they name: `block_map`: each group's row is a permutation of 0 to 7; codes under 1024 / 256 are prompt blocks, and the first and last block of every group hold prompt blocks.
All inputs are finite; a program needn't handle non-finite values.
Results may differ from the reference program's by a relative error of at most 0.017.
The reference program's roundings to bfloat16 on the way count: a program that leaves them out, or rounds other values in their place, can miss the bound.
Values may be sent and summed in bfloat16 or wider, within the bound.
No kernel may reach another device: no remote copies, remote signals or barrier semaphores. Data moves between devices by JAX's collectives and lax.ppermute only.
A program may use at most 640 MiB of HBM per device.

```python
import math
import jax
import jax.numpy as jnp
from jax import lax

D = 2048
HEADS = 32
HEAD_DIM = 64
FF = 5632
ROTARY = 16
CONT = 1024
BLOCK = 256
STEP = 10
GROUPS = 4
CYCLE = 8
GROUP_TOK = 2048
PROMPT = 1024
BLOCKS = 8
PARAMS = 51394560


def draw_block_map(key, part):
    key = jax.random.fold_in(key, 11)
    prompt_blocks = PROMPT // BLOCK

    def one(subkey):
        score_key, first_key, step_key = jax.random.split(subkey, 3)
        score = jax.random.permutation(score_key, BLOCKS).astype(jnp.int32)
        first = jax.random.randint(first_key, (), 0, prompt_blocks)
        stride = jax.random.randint(step_key, (), 1, prompt_blocks)
        last = (first + stride) % prompt_blocks
        codes = jnp.arange(BLOCKS, dtype=jnp.int32)
        score = jnp.where(codes == first, -1, score)
        score = jnp.where(codes == last, BLOCKS, score)
        return jnp.argsort(score, stable=True).astype(jnp.int32)
    return jax.vmap(one)(jax.random.split(key, GROUPS))


def draw_vectors(key, part):
    key = jax.random.fold_in(key, 23)
    wobble_key, shift_key = jax.random.split(key, 2)
    shard = D // (CYCLE * GROUPS)
    owner = jnp.arange(D, dtype=jnp.int32) // shard
    cycle_place = (owner // GROUPS).astype(jnp.float32) / max(CYCLE - 1, 1)
    group_place = (owner % GROUPS).astype(jnp.float32) / max(GROUPS - 1, 1)
    rise = 0.73
    base = 0.6
    wobble = jnp.exp(jax.random.uniform(wobble_key, (D, 2), minval=-0.22, maxval=0.22))
    shifts = jnp.clip(0.3 * jax.random.normal(shift_key, (D, 5)), -2.0, 2.0)
    gains = base * (1.0 + rise * cycle_place) * (1.0 + rise * group_place)
    gain_cols = gains[:, None] * wobble
    return jnp.stack([gain_cols[:, 0], shifts[:, 0], shifts[:, 1], shifts[:, 2], shifts[:, 3], gain_cols[:, 1], shifts[:, 4]], axis=1).astype(jnp.float32)


def shard_levels(rng, shape, cuts, smallest, largest):
    level = 1.0
    for axis_at, parts in cuts:
        draws = jax.random.uniform(jax.random.fold_in(jax.random.fold_in(rng, 6), axis_at), (parts,), jnp.float32, smallest / len(cuts), largest / len(cuts))
        level = level * jnp.repeat(jnp.exp(draws), shape[axis_at] // parts).reshape((-1,) + (1,) * (len(shape) - 1 - axis_at))
    return level


def bell_draw(rng, extent, deviation, bound, cuts=(), held_as=jnp.bfloat16):
    loudness = shard_levels(rng, extent, cuts, -0.22, 0.18) if cuts else 1.0
    drawn = jax.random.normal(rng, extent, jnp.float32) * deviation * loudness
    return jnp.minimum(jnp.maximum(drawn, -bound), bound).astype(held_as)


def setup_inputs(seed: int = 0) -> dict:
    arg_keys = jax.random.split(jax.random.key(seed), 19)
    layer_in = bell_draw(arg_keys[0], (GROUPS, GROUP_TOK, D), 1.0, 6.0, ((0, 4), (1, 8)))
    cotangent = bell_draw(arg_keys[1], (GROUPS, GROUP_TOK, D), 1.0, 6.0, ((0, 4), (1, 8)))
    block_map = draw_block_map(jax.random.fold_in(arg_keys[18], 71), 0)
    attn_in = bell_draw(arg_keys[3], (D, 3 * D), D ** -0.5, 0.125, ((0, 32),), jnp.float32)
    attn_out = bell_draw(arg_keys[4], (D, D), (max(D // 64, 32)) ** -0.5, 1.0, ((0, 32),), jnp.float32)
    ffn_in = bell_draw(arg_keys[5], (D, 2 * FF), D ** -0.5, 0.125, ((0, 32),), jnp.float32)
    ffn_out = bell_draw(arg_keys[6], (FF, D), (FF // 4) ** -0.5, 0.15625, ((0, 32),), jnp.float32)
    vectors = draw_vectors(jax.random.fold_in(arg_keys[18], 71), 0)
    first_attn_in = bell_draw(arg_keys[8], (D, 3 * D), (0.11 / PARAMS ** 0.5), 9.1552734375e-05, ((0, 32),), jnp.float32)
    first_attn_out = bell_draw(arg_keys[9], (D, D), (0.11 / PARAMS ** 0.5), 9.1552734375e-05, ((0, 32),), jnp.float32)
    first_ffn_in = bell_draw(arg_keys[10], (D, 2 * FF), (0.11 / PARAMS ** 0.5), 9.1552734375e-05, ((0, 32),), jnp.float32)
    first_ffn_out = bell_draw(arg_keys[11], (FF, D), (0.11 / PARAMS ** 0.5), 9.1552734375e-05, ((0, 32),), jnp.float32)
    first_vectors = bell_draw(arg_keys[12], (D, 7), (0.11 / PARAMS ** 0.5), 9.1552734375e-05, ((0, 32),), jnp.float32)
    second_attn_in = jnp.clip(jnp.exp(math.log(3.89146226353887e-09) - 1.3862944 * jax.random.uniform(arg_keys[13], (D, 3 * D), jnp.float32) ** shard_levels(arg_keys[13], (D, 3 * D), ((0, 32),), -0.2, 0.2)), 9.728655658847174e-10, 3.89146226353887e-09)
    second_attn_out = jnp.clip(jnp.exp(math.log(3.89146226353887e-09) - 1.3862944 * jax.random.uniform(arg_keys[14], (D, D), jnp.float32) ** shard_levels(arg_keys[14], (D, D), ((0, 32),), -0.2, 0.2)), 9.728655658847174e-10, 3.89146226353887e-09)
    second_ffn_in = jnp.clip(jnp.exp(math.log(3.89146226353887e-09) - 1.3862944 * jax.random.uniform(arg_keys[15], (D, 2 * FF), jnp.float32) ** shard_levels(arg_keys[15], (D, 2 * FF), ((0, 32),), -0.2, 0.2)), 9.728655658847174e-10, 3.89146226353887e-09)
    second_ffn_out = jnp.clip(jnp.exp(math.log(3.89146226353887e-09) - 1.3862944 * jax.random.uniform(arg_keys[16], (FF, D), jnp.float32) ** shard_levels(arg_keys[16], (FF, D), ((0, 32),), -0.2, 0.2)), 9.728655658847174e-10, 3.89146226353887e-09)
    second_vectors = jnp.clip(jnp.exp(math.log(3.89146226353887e-09) - 1.3862944 * jax.random.uniform(arg_keys[17], (D, 7), jnp.float32) ** shard_levels(arg_keys[17], (D, 7), ((0, 32),), -0.2, 0.2)), 9.728655658847174e-10, 3.89146226353887e-09)
    return dict(layer_in=layer_in, cotangent=cotangent, block_map=block_map, attn_in=attn_in, attn_out=attn_out, ffn_in=ffn_in, ffn_out=ffn_out, vectors=vectors, first_attn_in=first_attn_in, first_attn_out=first_attn_out, first_ffn_in=first_ffn_in, first_ffn_out=first_ffn_out, first_vectors=first_vectors, second_attn_in=second_attn_in, second_attn_out=second_attn_out, second_ffn_in=second_ffn_in, second_ffn_out=second_ffn_out, second_vectors=second_vectors)


HIGH = lax.Precision.HIGHEST
NORM_EPS = 1e-05
BETA_ONE = 0.9
BETA_TWO = 0.95
ADAM_EPS = 1e-08
DECAY = 0.1
CLIP_LIMIT = 1.0
ROPE_BASE = 10000.0
MASKED = -1e+30

@jax.custom_vjp
def low(v):
    return lax.optimization_barrier(v.astype(jnp.bfloat16)).astype(jnp.float32)

@jax.custom_vjp
def low_back(v):
    return v

def low_keep(v):
    return (low(v), None)

def low_pass(kept, grad):
    return (grad,)

def back_keep(v):
    return (v, None)

def back_low(kept, grad):
    return (low(grad),)
low.defvjp(low_keep, low_pass)
low_back.defvjp(back_keep, back_low)

def layout(codes):
    spread = jnp.repeat(codes, BLOCK, total_repeat_length=GROUP_TOK)
    inner = jnp.arange(GROUP_TOK, dtype=jnp.int32) % BLOCK
    prompt_blocks = PROMPT // BLOCK
    later = CONT // BLOCK
    offset = spread - prompt_blocks
    is_prompt = spread < prompt_blocks
    segments = jnp.where(is_prompt, 0, offset // later + 1).astype(jnp.int32)
    positions = jnp.where(is_prompt, spread * BLOCK + inner, PROMPT + offset % later * BLOCK + inner).astype(jnp.int32)
    return (segments, positions)

def layer_norm(values, gain, shift):
    center = values - lax.optimization_barrier(jnp.mean(values, axis=-1, keepdims=True))
    scaled = lax.rsqrt(lax.optimization_barrier(jnp.mean(center * center, axis=-1, keepdims=True)) + NORM_EPS)
    return center * scaled * gain + shift

def angles(positions):
    half = ROTARY // 2
    freq = jnp.power(ROPE_BASE, -2.0 * jnp.arange(half, dtype=jnp.float32) / ROTARY)
    turn = positions.astype(jnp.float32)[:, None] * freq[None, :]
    return (jnp.cos(turn), jnp.sin(turn))

def rotate(field, cosine, sine):
    half = cosine.shape[1]
    cosine = cosine[:, None, :]
    sine = sine[:, None, :]
    first = field[..., :half]
    second = field[..., half:2 * half]
    return jnp.concatenate([first * cosine - second * sine, second * cosine + first * sine, field[..., 2 * half:]], axis=-1)

def attend_group(query, keys, values, segments, positions):
    span = math.gcd(512, GROUP_TOK)
    blocks = GROUP_TOK // span
    scale = HEAD_DIM ** (-0.5)

    def one(pieces):
        block_query, block_seg, block_pos = pieces
        logits = jnp.einsum('qhd,khd->hqk', block_query, keys, precision=HIGH) * scale
        logits = low_back(logits)
        allowed = (positions[None, :] <= block_pos[:, None]) & ((segments[None, :] == block_seg[:, None]) | (segments[None, :] == 0))
        logits = jnp.where(allowed[None], logits, MASKED)
        top = lax.optimization_barrier(jnp.max(logits, axis=-1, keepdims=True))
        expo = jnp.exp(logits - top)
        probs = low(expo / lax.optimization_barrier(jnp.sum(expo, axis=-1, keepdims=True)))
        return jnp.einsum('hqk,khd->qhd', probs, values, precision=HIGH)
    mixed = lax.map(jax.checkpoint(one), (query.reshape(blocks, span, HEADS, HEAD_DIM), segments.reshape(blocks, span), positions.reshape(blocks, span)))
    return mixed.reshape(GROUP_TOK, HEADS, HEAD_DIM)

def forward(inputs, attn_in, attn_out, ffn_in, ffn_out, vectors, segments, positions):
    w_qkv = low(attn_in)
    w_attn = low(attn_out)
    w_up = low(ffn_in)
    w_down = low(ffn_out)
    vec = low(vectors)
    flat = inputs.reshape(GROUPS * GROUP_TOK, D)
    attn_act = low(layer_norm(flat, vec[:, 0], vec[:, 1]))
    bias = jnp.concatenate([vec[:, 2], vec[:, 3], vec[:, 4]])
    project = low_back(jnp.dot(attn_act, w_qkv, precision=HIGH, preferred_element_type=jnp.float32) + bias)
    cosine, sine = angles(positions.reshape(-1))
    query = low(rotate(project[:, :D].reshape(-1, HEADS, HEAD_DIM), cosine, sine))
    keys = low(rotate(project[:, D:2 * D].reshape(-1, HEADS, HEAD_DIM), cosine, sine))
    values = low(project[:, 2 * D:].reshape(-1, HEADS, HEAD_DIM))

    def group(pieces):
        return attend_group(*pieces)
    shape = (GROUPS, GROUP_TOK, HEADS, HEAD_DIM)
    mixed = lax.map(group, (query.reshape(shape), keys.reshape(shape), values.reshape(shape), segments, positions))
    mixed = low(low_back(mixed.reshape(-1, D)))
    resid = flat + low_back(jnp.dot(mixed, w_attn, precision=HIGH, preferred_element_type=jnp.float32))
    ffn_act = low(layer_norm(resid, vec[:, 5], vec[:, 6]))
    both = low_back(jnp.dot(ffn_act, w_up, precision=HIGH, preferred_element_type=jnp.float32))
    hidden = low(jax.nn.silu(both[:, :FF]) * both[:, FF:])
    result = resid + low_back(jnp.dot(hidden, w_down, precision=HIGH, preferred_element_type=jnp.float32))
    return result.reshape(GROUPS, GROUP_TOK, D)

def adam(weight, grad, first, second, rate):
    first = BETA_ONE * first + (1.0 - BETA_ONE) * grad
    second = BETA_TWO * second + (1.0 - BETA_TWO) * grad * grad
    fixed_first = first / (1.0 - BETA_ONE ** STEP)
    fixed_second = second / (1.0 - BETA_TWO ** STEP)
    weight = weight - rate * (fixed_first / (jnp.sqrt(fixed_second) + ADAM_EPS) + DECAY * weight)
    return (weight, first, second)

def reference(layer_in, cotangent, block_map, attn_in, attn_out, ffn_in, ffn_out, vectors, first_attn_in, first_attn_out, first_ffn_in, first_ffn_out, first_vectors, second_attn_in, second_attn_out, second_ffn_in, second_ffn_out, second_vectors):
    segments, positions = jax.vmap(layout)(block_map)

    def run(inputs, one_w, two_w, three_w, four_w, five_w):
        return forward(inputs, one_w, two_w, three_w, four_w, five_w, segments, positions)
    result, pullback = jax.vjp(run, layer_in.astype(jnp.float32), attn_in, attn_out, ffn_in, ffn_out, vectors)
    grads = pullback(cotangent.astype(jnp.float32))
    input_grad = grads[0]
    weight_grads = grads[1:]
    total = jnp.float32(0.0)
    for grad in weight_grads:
        total = total + jnp.sum(grad * grad)
    grad_norm = jnp.sqrt(total)
    clip = jnp.minimum(1.0, CLIP_LIMIT / (grad_norm + 1e-06))
    rates = (D ** (-0.5), 0.6 * max(D // 64, 32) ** (-0.5), D ** (-0.5), (FF // 4) ** (-0.5), 0.3)
    weights = (attn_in, attn_out, ffn_in, ffn_out, vectors)
    firsts = (first_attn_in, first_attn_out, first_ffn_in, first_ffn_out, first_vectors)
    seconds = (second_attn_in, second_attn_out, second_ffn_in, second_ffn_out, second_vectors)
    updated = []
    for index in range(5):
        updated.append(adam(weights[index], clip * weight_grads[index], firsts[index], seconds[index], rates[index]))
    return (result.astype(jnp.bfloat16), input_grad, grad_norm, updated[0][0], updated[0][1], updated[0][2], updated[1][0], updated[1][1], updated[1][2], updated[2][0], updated[2][1], updated[2][2], updated[3][0], updated[3][1], updated[3][2], updated[4][0], updated[4][1], updated[4][2])
```

```python
import functools
import math

import jax
import jax.numpy as jnp
from jax import lax
from jax.experimental import pallas as pl
from jax.experimental.pallas import tpu as pltpu
from jax.sharding import PartitionSpec as P

D = 2048
HEADS = 32
HEAD_DIM = 64
FF = 5632
ROTARY = 16
CONT = 1024
BLOCK = 256
STEP = 10

NORM_EPS = 1e-05
BETA_ONE = 0.9
BETA_TWO = 0.95
ADAM_EPS = 1e-08
DECAY = 0.1
CLIP_LIMIT = 1.0
ROPE_BASE = 10000.0
MASKED = -1e30
LANES = 128
SCALE = HEAD_DIM**-0.5
SCALE_LOG2 = SCALE * math.log2(math.e)
VMEM_LIMIT = 52 * 1024 * 1024
BF16 = jnp.bfloat16
F32 = jnp.float32

ORDER = (0, 2, 4, 6, 1, 3, 5, 7)


def standardize(values):
    center = values - jnp.mean(values, axis=-1, keepdims=True)
    scaled = lax.rsqrt(jnp.mean(center * center, axis=-1, keepdims=True) + NORM_EPS)
    return (center * scaled, scaled)


def norm_back(grad_normed, normed, scaled):
    return scaled * (
        grad_normed
        - jnp.mean(grad_normed, axis=-1, keepdims=True)
        - normed * jnp.mean(grad_normed * normed, axis=-1, keepdims=True)
    )


def adam(weight, grad, first, second, rate):
    first = BETA_ONE * first + (1.0 - BETA_ONE) * grad
    second = BETA_TWO * second + (1.0 - BETA_TWO) * grad * grad
    fixed_first = first / (1.0 - BETA_ONE**STEP)
    fixed_second = second / (1.0 - BETA_TWO**STEP)
    weight = weight - rate * (fixed_first / (jnp.sqrt(fixed_second) + ADAM_EPS) + DECAY * weight)
    return (weight, first, second)


def dot(left, right, left_dim, right_dim):
    return lax.dot_general(
        left, right, (((left_dim,), (right_dim,)), ((), ())), preferred_element_type=F32
    )


def swap(value, bit, axis="ctx"):
    size = lax.axis_size(axis)
    return lax.ppermute(value, axis, [(i, i ^ bit) for i in range(size)])


def cube():
    return lax.axis_size("ctx") == 8


def places():
    size = lax.axis_size("ctx")
    if cube():
        return lax.axis_index("ctx") ^ jnp.array(ORDER, jnp.int32)
    return jnp.arange(size, dtype=jnp.int32)


def gather_tokens(own):
    if not cube():
        return lax.all_gather(own, "ctx", axis=0, tiled=True)
    half = own.shape[0] // 2
    top, low = own[:half], own[half:]
    x_top = swap(top, 2)
    y_low = swap(low, 4)
    x_low = swap(low, 2)
    y_top = swap(top, 4)
    d_top = swap(x_top, 4)
    d_low = swap(y_low, 2)
    first = jnp.concatenate([own, x_top, x_low, y_top, y_low, d_top, d_low], axis=0)
    pieces = [own, x_top, x_low, y_top, y_low, d_top, d_low]
    other = [swap(piece, 1) for piece in pieces]
    return jnp.concatenate([first] + other, axis=0)


def scatter_tokens(make):
    size = lax.axis_size("ctx")
    if not cube():
        return lax.psum_scatter(
            make(0, size * BLOCK).astype(BF16), "ctx", scatter_dimension=0, tiled=True
        ).astype(F32)
    half = BLOCK // 2
    away = make(4 * BLOCK, 8 * BLOCK).astype(BF16)
    near = make(0, 4 * BLOCK)
    total = near + swap(away, 1).astype(F32)
    own = total[:BLOCK]
    x_part = total[BLOCK : 2 * BLOCK]
    y_part = total[2 * BLOCK : 3 * BLOCK]
    diag = total[3 * BLOCK :].astype(BF16)
    d_top = swap(diag[:half], 2).astype(F32)
    d_low = swap(diag[half:], 4).astype(F32)
    x_top = swap(x_part[:half].astype(BF16), 2).astype(F32)
    y_low = swap(y_part[half:].astype(BF16), 4).astype(F32)
    x_low = swap((x_part[half:] + d_low).astype(BF16), 2).astype(F32)
    y_top = swap((y_part[:half] + d_top).astype(BF16), 4).astype(F32)
    return own + jnp.concatenate([x_top + y_top, x_low + y_low], axis=0)


def sum_everywhere(value):
    for axis in ("ctx", "fsdp"):
        bit = 1
        while bit < lax.axis_size(axis):
            value = value + swap(value, bit, axis)
            bit *= 2
    return value


def aligned(index, step=BLOCK):
    return pl.ds(pl.multiple_of(index * step, step), step)


def turn(field, cosine, sine):
    lane = lax.broadcasted_iota(jnp.int32, field.shape, 1) % HEAD_DIM
    half = ROTARY // 2
    partner = jnp.where(
        lane < half, pltpu.roll(field, LANES - half, 1), pltpu.roll(field, half, 1)
    )
    return field * cosine + partner * sine


def full_blocks(code, prompt_blocks):
    later = CONT // BLOCK
    inside = lax.rem(code - prompt_blocks, later)
    return jnp.where(code < prompt_blocks, code, prompt_blocks + inside)


def key_block(code, index, prompt_blocks):
    later = CONT // BLOCK
    start = code - lax.rem(code - prompt_blocks, later)
    shifted = start + index - prompt_blocks
    return jnp.where(index < prompt_blocks, index, shifted)


def transposed(value):
    return value.astype(F32).T.astype(BF16)


def split_rows(pair):
    zero = jnp.zeros((HEAD_DIM, pair.shape[1]), pair.dtype)
    return (
        jnp.concatenate([pair[:HEAD_DIM], zero], axis=0),
        jnp.concatenate([zero, pair[HEAD_DIM:]], axis=0),
    )


def causal():
    key = lax.broadcasted_iota(jnp.int32, (BLOCK, BLOCK), 0)
    query = lax.broadcasted_iota(jnp.int32, (BLOCK, BLOCK), 1)
    return key <= query


def attend_kernel(
    pairs, blocks, inv_ref, proj_ref, bias_ref, cos_ref, sin_ref, q_ref, k_ref, v_ref, mix_ref, lse_ref, vt_ref
):
    prompt_blocks = blocks // 2
    wide = pairs * LANES
    lanes = [slice(p * LANES, (p + 1) * LANES) for p in range(pairs)]

    def prepare(code, carry):
        rows = aligned(inv_ref[code])
        place = aligned(code)
        cosine = cos_ref[place, :]
        sine = sin_ref[place, :]
        for p in range(pairs):
            at = [slice(part * wide + p * LANES, part * wide + (p + 1) * LANES) for part in range(3)]
            field = [proj_ref[rows, a] + bias_ref[:, a] for a in at]
            q_ref[place, lanes[p]] = turn(field[0], cosine, sine).astype(BF16)
            k_ref[place, lanes[p]] = turn(field[1], cosine, sine).astype(BF16)
            v_ref[place, lanes[p]] = field[2].astype(BF16)
            vt_ref[lanes[p], place] = field[2].T.astype(BF16)
        return carry

    lax.fori_loop(0, blocks, prepare, 0)
    allowed = causal()

    def one_query(code, carry):
        place = aligned(code)
        rows = aligned(inv_ref[code])
        heads = []
        for p in range(pairs):
            heads.extend(split_rows(transposed(q_ref[place, lanes[p]])))

        def scores(h, at):
            return dot(k_ref[at, lanes[h // 2]], heads[h], 1, 0) * SCALE_LOG2

        def mixing(h, at, probs):
            return dot(
                vt_ref[h * HEAD_DIM : (h + 1) * HEAD_DIM, at], probs.astype(BF16), 1, 0
            )

        state = []
        for h in range(2 * pairs):
            logits = jnp.where(allowed, scores(h, place), MASKED)
            top = jnp.max(logits, axis=0, keepdims=True)
            probs = jnp.exp2(logits - top)
            state.append((top, jnp.sum(probs, axis=0, keepdims=True), mixing(h, place, probs)))

        def step(index, state):
            at = aligned(key_block(code, index, prompt_blocks))
            fresh = []
            for h in range(2 * pairs):
                top, total, mixed = state[h]
                logits = scores(h, at)
                higher = jnp.maximum(top, jnp.max(logits, axis=0, keepdims=True))
                probs = jnp.exp2(logits - higher)
                fade = jnp.exp2(top - higher)
                fresh.append(
                    (
                        higher,
                        total * fade + jnp.sum(probs, axis=0, keepdims=True),
                        mixed * fade + mixing(h, at, probs),
                    )
                )
            return tuple(fresh)

        state = lax.fori_loop(0, full_blocks(code, prompt_blocks), step, tuple(state))
        for p in range(pairs):
            both = []
            for h in (2 * p, 2 * p + 1):
                top, total, mixed = state[h]
                both.append(mixed / total)
                lse_ref[h : h + 1, place] = top + jnp.log2(total)
            mix_ref[rows, lanes[p]] = jnp.concatenate(both, axis=0).T.astype(BF16)
        return carry

    lax.fori_loop(0, blocks, one_query, 0)


def attend(inv, project, bias, cosine, sine, pairs, blocks):
    tokens = blocks * BLOCK
    wide = pairs * LANES
    vmem = pl.BlockSpec(memory_space=pltpu.VMEM)
    low = jax.ShapeDtypeStruct((tokens, wide), BF16)
    return pl.pallas_call(
        functools.partial(attend_kernel, pairs, blocks),
        out_shape=(low, low, low, low, jax.ShapeDtypeStruct((2 * pairs, tokens), F32)),
        in_specs=[pl.BlockSpec(memory_space=pltpu.SMEM)] + [vmem] * 4,
        out_specs=(vmem,) * 5,
        scratch_shapes=[pltpu.VMEM((wide, tokens), BF16)],
        compiler_params=pltpu.CompilerParams(vmem_limit_bytes=VMEM_LIMIT),
        cost_estimate=pl.CostEstimate(
            flops=20 * pairs * tokens * tokens * HEAD_DIM,
            bytes_accessed=tokens * wide * 20,
            transcendentals=pairs * tokens * tokens,
        ),
        name="attend",
    )(inv, project, bias, cosine, sine)


def attend_back_kernel(
    pairs, blocks, inv_ref, q_ref, k_ref, v_ref, do_ref, lse_ref, cos_ref, sin_ref, gp_ref, kt_ref, dk_ref, dv_ref, p_ref, dp_ref
):
    prompt_blocks = blocks // 2
    wide = pairs * LANES
    lanes = [slice(p * LANES, (p + 1) * LANES) for p in range(pairs)]
    count = 2 * pairs

    def prepare(code, carry):
        place = aligned(code)
        for p in range(pairs):
            kt_ref[lanes[p], place] = transposed(k_ref[place, lanes[p]])
            zero = jnp.zeros((BLOCK, LANES), F32)
            dk_ref[place, lanes[p]] = zero
            dv_ref[place, lanes[p]] = zero
        return carry

    lax.fori_loop(0, blocks, prepare, 0)
    allowed = causal()
    lane = lax.broadcasted_iota(jnp.int32, (BLOCK, LANES), 1)

    def one_query(code, carry):
        place = aligned(code)
        rows = aligned(inv_ref[code])
        q_heads, do_heads, q_rows, do_rows = [], [], [], []
        for p in range(pairs):
            query = q_ref[place, lanes[p]]
            grad = do_ref[rows, lanes[p]]
            q_heads.extend(split_rows(transposed(query)))
            do_heads.extend(split_rows(transposed(grad)))
            for h in range(2):
                mine = (lane >= h * HEAD_DIM) & (lane < (h + 1) * HEAD_DIM)
                q_rows.append(jnp.where(mine, query, jnp.zeros_like(query)))
                do_rows.append(jnp.where(mine, grad, jnp.zeros_like(grad)))

        def probs_and_grads(slot, at, mask, sums):
            fresh = []
            for h in range(count):
                logits = dot(k_ref[at, lanes[h // 2]], q_heads[h], 1, 0) * SCALE_LOG2
                probs = jnp.exp2(logits - lse_ref[h : h + 1, place])
                if mask is not None:
                    probs = jnp.where(mask, probs, 0.0)
                grads = dot(v_ref[at, lanes[h // 2]], do_heads[h], 1, 0)
                p_ref[h, aligned(slot), :] = probs
                dp_ref[h, aligned(slot), :] = grads
                fresh.append(sums[h] + jnp.sum(probs * grads, axis=0, keepdims=True))
            return tuple(fresh)

        full = full_blocks(code, prompt_blocks)
        sums = probs_and_grads(full, place, allowed, (jnp.zeros((1, BLOCK), F32),) * count)
        sums = lax.fori_loop(
            0,
            full,
            lambda index, sums: probs_and_grads(
                index, aligned(key_block(code, index, prompt_blocks)), None, sums
            ),
            sums,
        )

        def step(index, grads):
            at = aligned(jnp.where(index == full, code, key_block(code, index, prompt_blocks)))
            fresh = []
            for p in range(pairs):
                for_key = dk_ref[at, lanes[p]]
                for_value = dv_ref[at, lanes[p]]
                for h in (2 * p, 2 * p + 1):
                    probs = p_ref[h, aligned(index), :]
                    low = (probs * (dp_ref[h, aligned(index), :] - sums[h])).astype(BF16)
                    for_key += dot(low, q_rows[h], 1, 0)
                    for_value += dot(probs.astype(BF16), do_rows[h], 1, 0)
                    fresh.append(
                        grads[h]
                        + dot(kt_ref[h * HEAD_DIM : (h + 1) * HEAD_DIM, at], low, 1, 0)
                    )
                dk_ref[at, lanes[p]] = for_key
                dv_ref[at, lanes[p]] = for_value
            return tuple(fresh)

        grads = lax.fori_loop(
            0, full + 1, step, (jnp.zeros((HEAD_DIM, BLOCK), F32),) * count
        )
        for p in range(pairs):
            pair = jnp.concatenate([grads[2 * p], grads[2 * p + 1]], axis=0).T * SCALE
            gp_ref[rows, lanes[p]] = turn(pair, cos_ref[place, :], -sin_ref[place, :]).astype(BF16)
        return carry

    lax.fori_loop(0, blocks, one_query, 0)

    def finish(code, carry):
        place = aligned(code)
        rows = aligned(inv_ref[code])
        for p in range(pairs):
            pair = dk_ref[place, lanes[p]] * SCALE
            at = slice(wide + p * LANES, wide + (p + 1) * LANES)
            gp_ref[rows, at] = turn(pair, cos_ref[place, :], -sin_ref[place, :]).astype(BF16)
            at = slice(2 * wide + p * LANES, 2 * wide + (p + 1) * LANES)
            gp_ref[rows, at] = dv_ref[place, lanes[p]].astype(BF16)
        return carry

    lax.fori_loop(0, blocks, finish, 0)


def attend_back(inv, query, key, value, grad, lse, cosine, sine, pairs, blocks):
    tokens = blocks * BLOCK
    wide = pairs * LANES
    vmem = pl.BlockSpec(memory_space=pltpu.VMEM)
    return pl.pallas_call(
        functools.partial(attend_back_kernel, pairs, blocks),
        out_shape=jax.ShapeDtypeStruct((tokens, 3 * wide), BF16),
        in_specs=[pl.BlockSpec(memory_space=pltpu.SMEM)] + [vmem] * 7,
        out_specs=vmem,
        scratch_shapes=[
            pltpu.VMEM((wide, tokens), BF16),
            pltpu.VMEM((tokens, wide), F32),
            pltpu.VMEM((tokens, wide), F32),
            pltpu.VMEM((2 * pairs, tokens, BLOCK), F32),
            pltpu.VMEM((2 * pairs, tokens, BLOCK), F32),
        ],
        compiler_params=pltpu.CompilerParams(vmem_limit_bytes=VMEM_LIMIT),
        cost_estimate=pl.CostEstimate(
            flops=60 * pairs * tokens * tokens * HEAD_DIM,
            bytes_accessed=tokens * wide * 20,
            transcendentals=pairs * tokens * tokens,
        ),
        name="attend_back",
    )(inv, query, key, value, grad, lse, cosine, sine)


def turn_tables(blocks):
    prompt_blocks = blocks // 2
    later = CONT // BLOCK
    token = jnp.arange(blocks * BLOCK, dtype=jnp.int32)
    code = token // BLOCK
    inner = token % BLOCK
    place = jnp.where(
        code < prompt_blocks,
        token,
        prompt_blocks * BLOCK + (code - prompt_blocks) % later * BLOCK + inner,
    )
    half = ROTARY // 2
    freq = jnp.power(ROPE_BASE, -2.0 * jnp.arange(half, dtype=F32) / ROTARY)
    angle = place.astype(F32)[:, None] * freq[None, :]
    cosine, sine = jnp.cos(angle), jnp.sin(angle)
    rest = HEAD_DIM - ROTARY
    ones = jnp.ones((blocks * BLOCK, rest), F32)
    one_cos = jnp.concatenate([cosine, cosine, ones], axis=1)
    one_sin = jnp.concatenate([-sine, sine, 0.0 * ones], axis=1)
    return (jnp.tile(one_cos, (1, 2)), jnp.tile(one_sin, (1, 2)))


def local(
    layer_in,
    cotangent,
    block_map,
    attn_in,
    attn_out,
    ffn_in,
    ffn_out,
    vectors,
    first_attn_in,
    first_attn_out,
    first_ffn_in,
    first_ffn_out,
    first_vectors,
    second_attn_in,
    second_attn_out,
    second_ffn_in,
    second_ffn_out,
    second_vectors,
):
    cycle = lax.axis_size("ctx")
    groups = lax.axis_size("fsdp")
    here = lax.axis_index("ctx")
    owner = here * groups + lax.axis_index("fsdp")
    blocks = block_map.shape[1]
    rows = attn_in.shape[0]
    wide = D // cycle
    pairs = wide // LANES
    units = FF // cycle
    padded = (units + LANES - 1) // LANES * LANES
    gap = padded - units

    mine = vectors.astype(BF16).T
    vec = lax.dynamic_update_slice(jnp.zeros((7, D), BF16), mine, (0, owner * rows))
    vec = sum_everywhere(vec).astype(F32)

    def spread(weight, parts):
        width = weight.shape[1] // (parts * cycle)
        split = weight.astype(BF16).reshape(rows, parts, cycle, width)
        split = split.transpose(2, 0, 1, 3).reshape(cycle, rows, parts * width)
        return lax.all_to_all(split, "ctx", 0, 0)

    def rows_of(split):
        full = lax.all_gather(split, "fsdp", axis=0, tiled=False)
        return full.transpose(1, 0, 2, 3).reshape(D, split.shape[2])

    w_qkv = rows_of(spread(attn_in, 3))
    w_attn = lax.all_gather(attn_out.astype(BF16), "fsdp", axis=0, tiled=True)
    both_in = rows_of(spread(ffn_in, 2))
    w_up = jnp.pad(both_in.reshape(D, 2, units), ((0, 0), (0, 0), (0, gap))).reshape(D, 2 * padded)
    w_down = lax.all_gather(ffn_out.astype(BF16), "fsdp", axis=0, tiled=True)
    w_down = jnp.pad(w_down, ((0, gap), (0, 0)))

    inputs = layer_in[0].astype(F32)
    normed_one, scaled_one = standardize(inputs)
    attn_act = gather_tokens((normed_one * vec[0] + vec[1]).astype(BF16))
    cot_low = gather_tokens(cotangent[0])
    codes = block_map[0][places()]
    inv = jnp.argsort(codes).astype(jnp.int32)
    cosine, sine = turn_tables(blocks)
    bias = lax.dynamic_slice_in_dim(vec[2:5], here * wide, wide, 1).reshape(1, 3 * wide)
    project = dot(attn_act, w_qkv, 1, 0)
    query, key, value, mixed, lse = attend(inv, project, bias, cosine, sine, pairs, blocks)
    resid = inputs + scatter_tokens(lambda a, b: dot(mixed[a:b], w_attn, 1, 0))

    normed_two, scaled_two = standardize(resid)
    ffn_act = gather_tokens((normed_two * vec[5] + vec[6]).astype(BF16))
    grad_hidden = dot(cot_low, w_down, 1, 1)
    both = dot(ffn_act, w_up, 1, 0)
    gate = both[:, :padded]
    upper = both[:, padded:]
    sigma = jax.nn.sigmoid(gate)
    active = gate * sigma
    hidden = (active * upper).astype(BF16)
    grad_gate = grad_hidden * upper * sigma * (1.0 + gate * (1.0 - sigma))
    grad_upper = grad_hidden * active
    grad_both = jnp.concatenate([grad_gate, grad_upper], axis=1).astype(BF16)
    grad_ffn_act = scatter_tokens(lambda a, b: dot(grad_both[a:b], w_up, 1, 1))

    def owners(grad):
        return lax.psum_scatter(grad, "fsdp", scatter_dimension=0, tiled=True).astype(F32)

    def owners_of_rows(grad):
        wider = grad.shape[1]
        split = grad.reshape(cycle, groups, rows, wider).transpose(1, 0, 2, 3)
        share = lax.psum_scatter(
            split.reshape(groups * cycle * rows, wider), "fsdp", scatter_dimension=0, tiled=True
        )
        return share.reshape(cycle, rows, wider)

    def collect(share, parts):
        width = share.shape[2] // parts
        split = lax.all_to_all(share, "ctx", 0, 0).reshape(cycle, rows, parts, width)
        return split.transpose(1, 2, 0, 3).reshape(rows, parts * cycle * width).astype(F32)

    grad_in = dot(ffn_act, grad_both, 0, 0).astype(BF16)
    grad_in = grad_in.reshape(D, 2, padded)[:, :, :units].reshape(D, 2 * units)
    share_in = owners_of_rows(grad_in)
    grad_down = dot(hidden, cot_low, 0, 0)[:units].astype(BF16)
    share_down = owners(grad_down)
    result = resid + scatter_tokens(lambda a, b: dot(hidden[a:b], w_down, 1, 0))
    layer_out = result.astype(BF16)[None]

    grad_resid = cotangent[0].astype(F32) + norm_back(
        grad_ffn_act * vec[5], normed_two, scaled_two
    )
    grad_branch = gather_tokens(grad_resid.astype(BF16))
    grad_mixed = dot(grad_branch, w_attn, 1, 1).astype(BF16)
    grad_project = attend_back(
        inv, query, key, value, grad_mixed, lse, cosine, sine, pairs, blocks
    )
    grad_attn_act = scatter_tokens(lambda a, b: dot(grad_project[a:b], w_qkv, 1, 1))
    input_grad = (grad_resid + norm_back(grad_attn_act * vec[0], normed_one, scaled_one))[None]
    share_out = owners(dot(mixed, grad_branch, 0, 0).astype(BF16))
    share_qkv = owners_of_rows(dot(attn_act, grad_project, 0, 0).astype(BF16))

    bias_grads = jnp.sum(grad_project.astype(F32), axis=0).reshape(3, wide)
    bias_grads = lax.dynamic_update_slice(jnp.zeros((3, D), F32), bias_grads, (0, here * wide))
    vector_grads = jnp.concatenate(
        [
            jnp.sum(grad_attn_act * normed_one, axis=0)[None],
            jnp.sum(grad_attn_act, axis=0)[None],
            bias_grads,
            jnp.sum(grad_ffn_act * normed_two, axis=0)[None],
            jnp.sum(grad_ffn_act, axis=0)[None],
        ],
        axis=0,
    )
    vector_grads = lax.dynamic_slice_in_dim(
        sum_everywhere(vector_grads), owner * rows, rows, 1
    ).T

    squares = F32(0.0)
    for grad in (share_qkv, share_out, share_in, share_down, vector_grads):
        wide_grad = grad.astype(F32)
        squares = squares + jnp.sum(wide_grad * wide_grad)
    grad_norm = jnp.sqrt(sum_everywhere(squares.reshape(1, 1)))[0, 0]
    clip = jnp.minimum(1.0, CLIP_LIMIT / (grad_norm + 1e-06))
    grad_list = (collect(share_qkv, 3), share_out, collect(share_in, 2), share_down, vector_grads)
    rates = (D ** (-0.5), 0.6 * max(D // 64, 32) ** (-0.5), D ** (-0.5), (FF // 4) ** (-0.5), 0.3)
    weights = (attn_in, attn_out, ffn_in, ffn_out, vectors)
    firsts = (first_attn_in, first_attn_out, first_ffn_in, first_ffn_out, first_vectors)
    seconds = (second_attn_in, second_attn_out, second_ffn_in, second_ffn_out, second_vectors)
    updated = []
    for index in range(5):
        updated.extend(
            adam(
                weights[index], clip * grad_list[index], firsts[index], seconds[index], rates[index]
            )
        )
    return (layer_out, input_grad, grad_norm, *updated)


def solution(mesh):
    tokens = P("fsdp", "ctx", None)
    owned = P(("ctx", "fsdp"), None)
    return jax.shard_map(
        local,
        mesh=mesh,
        in_specs=(tokens, tokens, P("fsdp", None)) + (owned,) * 15,
        out_specs=(tokens, tokens, P()) + (owned,) * 15,
        check_vma=False,
    )
```

```python
import functools
import math

import jax
import jax.numpy as jnp
from jax import lax
from jax.experimental import pallas as pl
from jax.experimental.pallas import tpu as pltpu
from jax.sharding import PartitionSpec as P

D = 2048
HEADS = 32
HEAD_DIM = 64
FF = 5632
ROTARY = 16
CONT = 1024
BLOCK = 256
STEP = 10

NORM_EPS = 1e-05
BETA_ONE = 0.9
BETA_TWO = 0.95
ADAM_EPS = 1e-08
DECAY = 0.1
CLIP_LIMIT = 1.0
ROPE_BASE = 10000.0
MASKED = -1e30
LANES = 128
SCALE = HEAD_DIM**-0.5
SCALE_LOG2 = SCALE * math.log2(math.e)
VMEM_LIMIT = 52 * 1024 * 1024
BF16 = jnp.bfloat16
SHORT = pl.CostEstimate(flops=1000000, bytes_accessed=1000000, transcendentals=0)
F32 = jnp.float32

ORDER = (0, 2, 4, 6, 1, 3, 5, 7)


def standardize(values):
    center = values - jnp.mean(values, axis=-1, keepdims=True)
    scaled = lax.rsqrt(jnp.mean(center * center, axis=-1, keepdims=True) + NORM_EPS)
    return (center * scaled, scaled)


def norm_back(grad_normed, normed, scaled):
    return scaled * (
        grad_normed
        - jnp.mean(grad_normed, axis=-1, keepdims=True)
        - normed * jnp.mean(grad_normed * normed, axis=-1, keepdims=True)
    )


def adam(weight, grad, first, second, rate):
    first = BETA_ONE * first + (1.0 - BETA_ONE) * grad
    second = BETA_TWO * second + (1.0 - BETA_TWO) * grad * grad
    fixed_first = first / (1.0 - BETA_ONE**STEP)
    fixed_second = second / (1.0 - BETA_TWO**STEP)
    weight = weight - rate * (fixed_first / (jnp.sqrt(fixed_second) + ADAM_EPS) + DECAY * weight)
    return (weight, first, second)


def dot(left, right, left_dim, right_dim):
    return lax.dot_general(
        left, right, (((left_dim,), (right_dim,)), ((), ())), preferred_element_type=F32
    )


def swap(value, bit, axis="ctx"):
    size = lax.axis_size(axis)
    return lax.ppermute(value, axis, [(i, i ^ bit) for i in range(size)])


def cube():
    return lax.axis_size("ctx") == 8


def places():
    size = lax.axis_size("ctx")
    if cube():
        return lax.axis_index("ctx") ^ jnp.array(ORDER, jnp.int32)
    return jnp.arange(size, dtype=jnp.int32)


def tie(*values):
    return lax.optimization_barrier(values)


def window(begun, *others):
    if not cube():
        return (begun, *others)
    tied = tie(*begun[-2:], *others)
    return (begun[:-2] + tied[:2], *tied[2:])


def gather_start(top, low):
    if not cube():
        return (lax.all_gather(jnp.concatenate([top, low]), "ctx", axis=0, tiled=True),)
    x_top = swap(top, 2)
    y_low = swap(low, 4)
    c_top = swap(top, 1)
    c_low = swap(low, 1)
    c_top, c_low, top, low = tie(c_top, c_low, top, low)
    return (top, low, c_top, c_low, x_top, y_low, swap(low, 2), swap(top, 4))


def gather_far(begun):
    if not cube():
        return ()
    return (swap(begun[4], 4), swap(begun[5], 2))


def gather_near(begun):
    top, low, c_top, c_low, x_top, y_low, x_low, y_top = begun
    near = (x_top, x_low, y_top, y_low)
    return (top, low, *near, c_top, c_low) + tuple(swap(piece, 1) for piece in near)


def gather_late(far):
    return far + tuple(swap(piece, 1) for piece in far)


def gather_pieces(begun, far=None):
    if not cube():
        return begun
    near = gather_near(begun)
    late = gather_late(gather_far(begun) if far is None else far)
    return near[:6] + late[:2] + near[6:] + late[2:]


def chip_kernel(right_dim, left_ref, right_ref, other_ref, own, x_top, x_low, y_top, y_low, d_top, d_low):
    total = dot(left_ref[...], right_ref[...], 1, right_dim) + other_ref[...].astype(F32)
    low = total.astype(BF16)
    half = BLOCK // 2

    @pl.when(pl.program_id(0) == 0)
    def _():
        own[...] = low[:BLOCK]
        x_top[...] = low[BLOCK : BLOCK + half]
        x_low[...] = low[BLOCK + half :]

    @pl.when(pl.program_id(0) == 1)
    def _():
        y_top[...] = low[:half]
        y_low[...] = low[half:BLOCK]
        d_top[...] = low[BLOCK : BLOCK + half]
        d_low[...] = low[BLOCK + half :]


def chip_sums(left, right, right_dim, other):
    depth = left.shape[1]
    half = BLOCK // 2
    cuts = (BLOCK,) + (half,) * 6
    return pl.pallas_call(
        functools.partial(chip_kernel, right_dim),
        grid=(2,),
        out_shape=tuple(jax.ShapeDtypeStruct((cut, D), BF16) for cut in cuts),
        in_specs=[
            pl.BlockSpec((2 * BLOCK, depth), lambda i: (i, 0)),
            pl.BlockSpec(right.shape, lambda i: (0, 0), pipeline_mode=pl.Buffered(1)),
            pl.BlockSpec((2 * BLOCK, D), lambda i: (i, 0)),
        ],
        out_specs=tuple(pl.BlockSpec((cut, D), lambda i: (0, 0)) for cut in cuts),
        compiler_params=pltpu.CompilerParams(vmem_limit_bytes=VMEM_LIMIT),
        cost_estimate=SHORT,
        name="chip_sums",
    )(left, right, other)


def scatter_away(left, right, right_dim):
    if not cube():
        return None
    return swap(dot(left[4 * BLOCK :], right, 1, right_dim).astype(BF16), 1)


def scatter_sums(left, right, right_dim, away):
    if not cube():
        part = dot(left, right, 1, right_dim).astype(BF16)
        return (lax.psum_scatter(part, "ctx", scatter_dimension=0, tiled=True),)
    return tuple(chip_sums(left, right, right_dim, away))


def scatter_start(sums):
    if not cube():
        return sums
    own, x_top, x_low, y_top, y_low, d_top, d_low = sums
    return (own, x_low, y_top, swap(d_top, 2), swap(d_low, 4), swap(x_top, 2), swap(y_low, 4))


def scatter_end(begun):
    if not cube():
        return begun
    own, x_low, y_top, d_top, d_low, x_top, y_low = begun
    x_low = swap((x_low.astype(F32) + d_low.astype(F32)).astype(BF16), 2)
    y_top = swap((y_top.astype(F32) + d_top.astype(F32)).astype(BF16), 4)
    return (own, x_top, y_top, x_low, y_low)


def total_of(parts):
    parts = [part.astype(F32) for part in parts]
    if len(parts) == 1:
        return parts[0]
    own, x_top, y_top, x_low, y_low = parts
    return own + jnp.concatenate([x_top + y_top, x_low + y_low], axis=0)


def split_kernel(parts, size, width, w_ref, *refs):
    rows = w_ref.shape[0]
    out_ref = refs[-1]
    for c in range(size):
        for p in range(parts):
            column = (p * size + c) * width
            block = w_ref[:, column : column + width].astype(BF16)
            out_ref[c, :rows, p * width : (p + 1) * width] = block
        if len(refs) > 1:
            out_ref[c, rows:, :] = refs[0][...]


def join_kernel(parts, size, width, share_ref, out_ref):
    for c in range(size):
        for p in range(parts):
            column = (p * size + c) * width
            out_ref[:, column : column + width] = share_ref[c, :, p * width : (p + 1) * width]


def relayout(kernel, values, shape, name):
    return pl.pallas_call(
        kernel,
        out_shape=jax.ShapeDtypeStruct(shape, BF16),
        in_specs=[pl.BlockSpec(memory_space=pltpu.VMEM)] * len(values),
        out_specs=pl.BlockSpec(memory_space=pltpu.VMEM),
        compiler_params=pltpu.CompilerParams(vmem_limit_bytes=VMEM_LIMIT),
        cost_estimate=SHORT,
        name=name,
    )(*values)


def split_columns(weight, parts, *below):
    size = lax.axis_size("ctx")
    rows = weight.shape[0]
    width = weight.shape[1] // (parts * size)
    if not cube():
        split = weight.astype(BF16).reshape(rows, parts, size, width)
        split = split.transpose(2, 0, 1, 3).reshape(size, rows, parts * width)
        below = [jnp.broadcast_to(value, (size, *value.shape)) for value in below]
        return jnp.concatenate([split, *below], axis=1)
    kernel = functools.partial(split_kernel, parts, size, width)
    total = rows + sum(value.shape[0] for value in below)
    return relayout(kernel, (weight, *below), (size, total, parts * width), "split_columns")


def join_columns(share, parts):
    size, rows, width = share.shape
    width = width // parts
    if not cube():
        split = share.reshape(size, rows, parts, width)
        return split.transpose(1, 2, 0, 3).reshape(rows, parts * size * width)
    kernel = functools.partial(join_kernel, parts, size, width)
    return relayout(kernel, (share,), (rows, parts * size * width), "join_columns")


def exchange(split):
    return lax.all_to_all(split, "ctx", 0, 0)


def sum_everywhere(value, axes=("ctx", "fsdp")):
    for axis in axes:
        bit = 1
        while bit < lax.axis_size(axis):
            value = value + swap(value, bit, axis)
            bit *= 2
    return value


def aligned(index, step=BLOCK):
    return pl.ds(pl.multiple_of(index * step, step), step)


def turn(field, cosine, sine):
    lane = lax.broadcasted_iota(jnp.int32, field.shape, 1) % HEAD_DIM
    half = ROTARY // 2
    partner = jnp.where(
        lane < half, pltpu.roll(field, LANES - half, 1), pltpu.roll(field, half, 1)
    )
    return field * cosine + partner * sine


def full_blocks(code, prompt_blocks):
    later = CONT // BLOCK
    inside = lax.rem(code - prompt_blocks, later)
    return jnp.where(code < prompt_blocks, code, prompt_blocks + inside)


def key_block(code, index, prompt_blocks):
    later = CONT // BLOCK
    start = code - lax.rem(code - prompt_blocks, later)
    shifted = start + index - prompt_blocks
    return jnp.where(index < prompt_blocks, index, shifted)


def transposed(value):
    return value.astype(F32).T.astype(BF16)


def fold(value):
    return value.reshape(value.shape[0] // 8, 8, value.shape[1])


def split_rows(pair):
    zero = jnp.zeros((HEAD_DIM, pair.shape[1]), pair.dtype)
    return (
        jnp.concatenate([pair[:HEAD_DIM], zero], axis=0),
        jnp.concatenate([zero, pair[HEAD_DIM:]], axis=0),
    )


def causal():
    key = lax.broadcasted_iota(jnp.int32, (BLOCK, BLOCK), 0)
    query = lax.broadcasted_iota(jnp.int32, (BLOCK, BLOCK), 1)
    return key <= query


def attend_kernel(
    pairs, blocks, inv_ref, proj_ref, bias_ref, cos_ref, sin_ref, q_ref, k_ref, v_ref, mix_ref, lse_ref, vt_ref, s_ref
):
    prompt_blocks = blocks // 2
    wide = pairs * LANES
    lanes = [slice(p * LANES, (p + 1) * LANES) for p in range(pairs)]
    count = 2 * pairs

    def prepare(code, carry):
        rows = aligned(inv_ref[code])
        place = aligned(code)
        cosine = cos_ref[place, :]
        sine = sin_ref[place, :]
        for p in range(pairs):
            at = [slice(part * wide + p * LANES, part * wide + (p + 1) * LANES) for part in range(3)]
            field = [proj_ref[rows, a] + bias_ref[:, a] for a in at]
            q_ref[place, lanes[p]] = turn(field[0], cosine, sine).astype(BF16)
            k_ref[place, lanes[p]] = turn(field[1], cosine, sine).astype(BF16)
            v_ref[place, lanes[p]] = field[2].astype(BF16)
            vt_ref[lanes[p], place] = field[2].T.astype(BF16)
        return carry

    lax.fori_loop(0, blocks, prepare, 0)
    allowed = causal()

    def one_query(code, carry):
        place = aligned(code)
        rows = aligned(inv_ref[code])
        heads = []
        for p in range(pairs):
            heads.extend(split_rows(transposed(q_ref[place, lanes[p]])))

        def scores(slot, at, mask, tops):
            fresh = []
            for h in range(count):
                logits = dot(k_ref[at, lanes[h // 2]], heads[h], 1, 0) * SCALE_LOG2
                if mask is not None:
                    logits = jnp.where(mask, logits, MASKED)
                s_ref[h, aligned(slot), :] = logits
                fresh.append(jnp.maximum(tops[h], jnp.max(fold(logits), axis=0)))
            return tuple(fresh)

        full = full_blocks(code, prompt_blocks)
        tops = scores(full, place, allowed, (jnp.full((8, BLOCK), MASKED, F32),) * count)
        tops = lax.fori_loop(
            0,
            full,
            lambda index, tops: scores(
                index, aligned(key_block(code, index, prompt_blocks)), None, tops
            ),
            tops,
        )
        tops = [jnp.max(top, axis=0, keepdims=True) for top in tops]

        def step(index, state):
            at = aligned(jnp.where(index == full, code, key_block(code, index, prompt_blocks)))
            fresh = []
            for h in range(count):
                total, mixed = state[h]
                probs = jnp.exp2(s_ref[h, aligned(index), :] - tops[h])
                total = total + jnp.sum(fold(probs), axis=0)
                mixed = mixed + dot(
                    vt_ref[h * HEAD_DIM : (h + 1) * HEAD_DIM, at], probs.astype(BF16), 1, 0
                )
                fresh.append((total, mixed))
            return tuple(fresh)

        state = ((jnp.zeros((8, BLOCK), F32), jnp.zeros((HEAD_DIM, BLOCK), F32)),) * count
        state = lax.fori_loop(0, full + 1, step, state)
        for p in range(pairs):
            both = []
            for h in (2 * p, 2 * p + 1):
                total, mixed = state[h]
                total = jnp.sum(total, axis=0, keepdims=True)
                both.append(mixed / total)
                lse_ref[h : h + 1, place] = tops[h] + jnp.log2(total)
            mix_ref[rows, lanes[p]] = jnp.concatenate(both, axis=0).T.astype(BF16)
        return carry

    lax.fori_loop(0, blocks, one_query, 0)


def attend(inv, project, bias, cosine, sine, pairs, blocks):
    tokens = blocks * BLOCK
    wide = pairs * LANES
    vmem = pl.BlockSpec(memory_space=pltpu.VMEM)
    low = jax.ShapeDtypeStruct((tokens, wide), BF16)
    return pl.pallas_call(
        functools.partial(attend_kernel, pairs, blocks),
        out_shape=(low, low, low, low, jax.ShapeDtypeStruct((2 * pairs, tokens), F32)),
        in_specs=[pl.BlockSpec(memory_space=pltpu.SMEM)] + [vmem] * 4,
        out_specs=(vmem,) * 5,
        scratch_shapes=[
            pltpu.VMEM((wide, tokens), BF16),
            pltpu.VMEM((2 * pairs, tokens, BLOCK), F32),
        ],
        compiler_params=pltpu.CompilerParams(vmem_limit_bytes=VMEM_LIMIT),
        cost_estimate=SHORT,
        name="attend",
    )(inv, project, bias, cosine, sine)


def attend_back_kernel(
    pairs, blocks, inv_ref, q_ref, k_ref, v_ref, do_ref, lse_ref, cos_ref, sin_ref, gp_ref, kt_ref, dk_ref, dv_ref, p_ref, dp_ref
):
    prompt_blocks = blocks // 2
    wide = pairs * LANES
    lanes = [slice(p * LANES, (p + 1) * LANES) for p in range(pairs)]
    count = 2 * pairs

    def prepare(code, carry):
        place = aligned(code)
        for p in range(pairs):
            kt_ref[lanes[p], place] = transposed(k_ref[place, lanes[p]])
            zero = jnp.zeros((BLOCK, LANES), F32)
            dk_ref[place, lanes[p]] = zero
            dv_ref[place, lanes[p]] = zero
        return carry

    lax.fori_loop(0, blocks, prepare, 0)
    allowed = causal()
    lane = lax.broadcasted_iota(jnp.int32, (BLOCK, LANES), 1)

    def one_query(code, carry):
        place = aligned(code)
        rows = aligned(inv_ref[code])
        q_heads, do_heads, q_rows, do_rows = [], [], [], []
        for p in range(pairs):
            query = q_ref[place, lanes[p]]
            grad = do_ref[rows, lanes[p]]
            q_heads.extend(split_rows(transposed(query)))
            do_heads.extend(split_rows(transposed(grad)))
            for h in range(2):
                mine = (lane >= h * HEAD_DIM) & (lane < (h + 1) * HEAD_DIM)
                q_rows.append(jnp.where(mine, query, jnp.zeros_like(query)))
                do_rows.append(jnp.where(mine, grad, jnp.zeros_like(grad)))

        def probs_and_grads(slot, at, mask, sums):
            fresh = []
            for h in range(count):
                logits = dot(k_ref[at, lanes[h // 2]], q_heads[h], 1, 0) * SCALE_LOG2
                probs = jnp.exp2(logits - lse_ref[h : h + 1, place])
                if mask is not None:
                    probs = jnp.where(mask, probs, 0.0)
                grads = dot(v_ref[at, lanes[h // 2]], do_heads[h], 1, 0)
                p_ref[h, aligned(slot), :] = probs
                dp_ref[h, aligned(slot), :] = grads
                fresh.append(sums[h] + jnp.sum(fold(probs * grads), axis=0))
            return tuple(fresh)

        full = full_blocks(code, prompt_blocks)
        sums = probs_and_grads(full, place, allowed, (jnp.zeros((8, BLOCK), F32),) * count)
        sums = lax.fori_loop(
            0,
            full,
            lambda index, sums: probs_and_grads(
                index, aligned(key_block(code, index, prompt_blocks)), None, sums
            ),
            sums,
        )
        sums = [jnp.sum(total, axis=0, keepdims=True) for total in sums]

        def step(index, grads):
            at = aligned(jnp.where(index == full, code, key_block(code, index, prompt_blocks)))
            fresh = []
            for p in range(pairs):
                for_key = dk_ref[at, lanes[p]]
                for_value = dv_ref[at, lanes[p]]
                for h in (2 * p, 2 * p + 1):
                    probs = p_ref[h, aligned(index), :]
                    low = (probs * (dp_ref[h, aligned(index), :] - sums[h])).astype(BF16)
                    for_key += dot(low, q_rows[h], 1, 0)
                    for_value += dot(probs.astype(BF16), do_rows[h], 1, 0)
                    fresh.append(
                        grads[h]
                        + dot(kt_ref[h * HEAD_DIM : (h + 1) * HEAD_DIM, at], low, 1, 0)
                    )
                dk_ref[at, lanes[p]] = for_key
                dv_ref[at, lanes[p]] = for_value
            return tuple(fresh)

        grads = lax.fori_loop(
            0, full + 1, step, (jnp.zeros((HEAD_DIM, BLOCK), F32),) * count
        )
        for p in range(pairs):
            pair = jnp.concatenate([grads[2 * p], grads[2 * p + 1]], axis=0).T * SCALE
            gp_ref[rows, lanes[p]] = turn(pair, cos_ref[place, :], -sin_ref[place, :]).astype(BF16)
        return carry

    lax.fori_loop(0, blocks, one_query, 0)

    def finish(code, carry):
        place = aligned(code)
        rows = aligned(inv_ref[code])
        for p in range(pairs):
            pair = dk_ref[place, lanes[p]] * SCALE
            at = slice(wide + p * LANES, wide + (p + 1) * LANES)
            gp_ref[rows, at] = turn(pair, cos_ref[place, :], -sin_ref[place, :]).astype(BF16)
            at = slice(2 * wide + p * LANES, 2 * wide + (p + 1) * LANES)
            gp_ref[rows, at] = dv_ref[place, lanes[p]].astype(BF16)
        return carry

    lax.fori_loop(0, blocks, finish, 0)


def attend_back(inv, query, key, value, grad, lse, cosine, sine, pairs, blocks):
    tokens = blocks * BLOCK
    wide = pairs * LANES
    vmem = pl.BlockSpec(memory_space=pltpu.VMEM)
    return pl.pallas_call(
        functools.partial(attend_back_kernel, pairs, blocks),
        out_shape=jax.ShapeDtypeStruct((tokens, 3 * wide), BF16),
        in_specs=[pl.BlockSpec(memory_space=pltpu.SMEM)] + [vmem] * 7,
        out_specs=vmem,
        scratch_shapes=[
            pltpu.VMEM((wide, tokens), BF16),
            pltpu.VMEM((tokens, wide), F32),
            pltpu.VMEM((tokens, wide), F32),
            pltpu.VMEM((2 * pairs, tokens, BLOCK), F32),
            pltpu.VMEM((2 * pairs, tokens, BLOCK), F32),
        ],
        compiler_params=pltpu.CompilerParams(vmem_limit_bytes=VMEM_LIMIT),
        cost_estimate=SHORT,
        name="attend_back",
    )(inv, query, key, value, grad, lse, cosine, sine)


def load_tile(pieces, out_ref, tile):
    start = 0
    for piece in pieces:
        cut = piece.shape[0]

        @pl.when(pl.program_id(0) == start // tile)
        def _(piece=piece, start=start % tile, cut=cut):
            out_ref[start : start + cut, :] = piece[...]

        start += cut


def whole(value):
    return pl.BlockSpec(value.shape, lambda i: (0, 0), pipeline_mode=pl.Buffered(1))


def norm_kernel(gain_ref, shift_ref, *refs):
    out_ref, held = refs[-2:]
    load_tile(refs[:-2], held, BLOCK)
    normed, _ = standardize(held[...].astype(F32))
    out_ref[...] = (normed * gain_ref[...] + shift_ref[...]).astype(BF16)


def norm_pieces(pieces, gain, shift):
    if not cube():
        return (standardize(pieces[0].astype(F32))[0] * gain + shift).astype(BF16)
    tokens = sum(piece.shape[0] for piece in pieces)
    values = (gain, shift, *pieces)
    return pl.pallas_call(
        norm_kernel,
        grid=(tokens // BLOCK,),
        out_shape=jax.ShapeDtypeStruct((tokens, D), BF16),
        in_specs=[whole(value) for value in values],
        out_specs=pl.BlockSpec((BLOCK, D), lambda i: (i, 0)),
        scratch_shapes=[pltpu.VMEM((BLOCK, D), BF16)],
        compiler_params=pltpu.CompilerParams(vmem_limit_bytes=VMEM_LIMIT),
        cost_estimate=SHORT,
        name="norm_pieces",
    )(*values)


def halves(value):
    half = value.shape[0] // 2
    return value[:half], value[half:]


def enter_feed(inputs, gain, shift, *parts):
    resid = inputs.astype(F32) + total_of(parts)
    normed, _ = standardize(resid)
    return (resid, *halves((normed * gain + shift).astype(BF16)))


def leave_feed(cotangent, resid, gain, *parts):
    grad = total_of(parts)
    normed, scaled = standardize(resid)
    grad_resid = cotangent.astype(F32) + norm_back(grad * gain, normed, scaled)
    sums = [jnp.sum(grad * normed, axis=0, keepdims=True), jnp.sum(grad, axis=0, keepdims=True)]
    return (grad_resid, *halves(grad_resid.astype(BF16)), *sums)


def leave_layer(inputs, grad_resid, gain, *parts):
    grad = total_of(parts)
    normed, scaled = standardize(inputs.astype(F32))
    sums = [jnp.sum(grad * normed, axis=0, keepdims=True), jnp.sum(grad, axis=0, keepdims=True)]
    return (grad_resid + norm_back(grad * gain, normed, scaled), *sums)


def own_kernel(step, count, *refs):
    results = step(*(ref[...] for ref in refs[:count]))
    for ref, result in zip(refs[count:], results):
        ref[...] = result


def own_rows(step, *values):
    if not cube():
        return step(*values)
    vmem = pl.BlockSpec(memory_space=pltpu.VMEM)
    shapes = jax.eval_shape(step, *values)
    return pl.pallas_call(
        functools.partial(own_kernel, step, len(values)),
        out_shape=shapes,
        in_specs=[vmem] * len(values),
        out_specs=tuple(vmem for _ in shapes),
        compiler_params=pltpu.CompilerParams(vmem_limit_bytes=VMEM_LIMIT),
        cost_estimate=SHORT,
        name=step.__name__,
    )(*values)


def ffn_up_kernel(units, count, w_ref, *refs):
    act_ref, both_ref, hidden_ref = refs[-3:]
    load_tile(refs[:count], act_ref, BLOCK)
    both_ref[...] = dot(act_ref[...], w_ref[...], 1, 0)
    gate = both_ref[:, :units]
    upper = both_ref[:, units:]
    hidden_ref[...] = (gate * jax.nn.sigmoid(gate) * upper).astype(BF16)


def ffn_up_step(pieces, weight, units, place, before):
    steps = sum(piece.shape[0] for piece in pieces) // BLOCK
    tokens = lax.axis_size("ctx") * BLOCK
    count = len(pieces)
    return pl.pallas_call(
        functools.partial(ffn_up_kernel, units, count),
        grid=(steps,),
        out_shape=(
            jax.ShapeDtypeStruct((tokens, D), BF16),
            jax.ShapeDtypeStruct((tokens, 2 * units), F32),
            jax.ShapeDtypeStruct((tokens, units), BF16),
        ),
        in_specs=[whole(weight)]
        + [whole(piece) for piece in pieces]
        + [pl.BlockSpec(memory_space=pl.ANY)] * len(before),
        out_specs=(
            pl.BlockSpec((BLOCK, D), lambda i: (place(i), 0)),
            pl.BlockSpec((BLOCK, 2 * units), lambda i: (place(i), 0)),
            pl.BlockSpec((BLOCK, units), lambda i: (place(i), 0)),
        ),
        input_output_aliases={1 + count + k: k for k in range(len(before))},
        compiler_params=pltpu.CompilerParams(vmem_limit_bytes=VMEM_LIMIT),
        cost_estimate=SHORT,
        name="ffn_up",
    )(weight, *pieces, *before)


def ffn_up(begun, weight, units):
    if not cube():
        act = begun[0]
        both = dot(act, weight, 1, 0)
        gate = both[:, :units]
        return act, both, (gate * jax.nn.sigmoid(gate) * both[:, units:]).astype(BF16)
    far = gather_far(begun)
    early = ffn_up_step(gather_near(begun), weight, units, lambda i: i + i // 3, ())
    far, early = tie(far, early)
    return ffn_up_step(gather_late(far), weight, units, lambda i: 3 + 4 * i, early)


def ffn_back_kernel(units, both_ref, cot_ref, down_ref, gb_ref):
    grad = dot(cot_ref[...], down_ref[...], 1, 1)
    gate = both_ref[:, :units]
    upper = both_ref[:, units:]
    sigma = jax.nn.sigmoid(gate)
    gb_ref[:, :units] = (grad * upper * sigma * (1.0 + gate * (1.0 - sigma))).astype(BF16)
    gb_ref[:, units:] = (grad * (gate * sigma)).astype(BF16)


def ffn_back(both, cot, down, units):
    if not cube():
        grad = dot(cot, down, 1, 1)
        gate = both[:, :units]
        sigma = jax.nn.sigmoid(gate)
        grad_gate = grad * both[:, units:] * sigma * (1.0 + gate * (1.0 - sigma))
        return jnp.concatenate([grad_gate, grad * (gate * sigma)], axis=1).astype(BF16)
    tokens = cot.shape[0]
    tile = 2 * BLOCK
    return pl.pallas_call(
        functools.partial(ffn_back_kernel, units),
        grid=(tokens // tile,),
        out_shape=jax.ShapeDtypeStruct((tokens, 2 * units), BF16),
        in_specs=[
            pl.BlockSpec((tile, 2 * units), lambda i: (i, 0)),
            pl.BlockSpec((tile, D), lambda i: (i, 0)),
            pl.BlockSpec((units, D), lambda i: (0, 0), pipeline_mode=pl.Buffered(1)),
        ],
        out_specs=pl.BlockSpec((tile, 2 * units), lambda i: (i, 0)),
        compiler_params=pltpu.CompilerParams(vmem_limit_bytes=VMEM_LIMIT),
        cost_estimate=SHORT,
        name="ffn_back",
    )(both, cot, down)


def branch_kernel(first, last, starts, mixed_ref, right_ref, *refs):
    count = len(starts)
    left_ref, grad_ref = refs[-2:]
    total = jnp.zeros(grad_ref.shape, F32)
    if not first:
        left_ref[...] = refs[count][...]
        total = refs[count + 1][...]
    for start, ref in zip(starts, refs):
        stop = start + ref.shape[0]
        left_ref[start:stop, :] = dot(ref[...], right_ref[...], 1, 1).astype(BF16)
        total += dot(mixed_ref[start:stop, :], ref[...], 0, 0)
    grad_ref[...] = total.astype(grad_ref.dtype)


def branch_step(mixed, right, pieces, starts, before, last):
    vmem = pl.BlockSpec(memory_space=pltpu.VMEM)
    values = (mixed, right, *pieces, *before)
    return pl.pallas_call(
        functools.partial(branch_kernel, not before, last, starts),
        out_shape=(
            jax.ShapeDtypeStruct(mixed.shape, BF16),
            jax.ShapeDtypeStruct((mixed.shape[1], D), BF16 if last else F32),
        ),
        in_specs=[vmem] * len(values),
        out_specs=(vmem, vmem),
        compiler_params=pltpu.CompilerParams(vmem_limit_bytes=VMEM_LIMIT),
        cost_estimate=SHORT,
        name="branch_step",
    )(*values)


def branch_grads(mixed, right, begun):
    if not cube():
        (whole_branch,) = begun
        left = dot(whole_branch, right, 1, 1).astype(BF16)
        return left, dot(mixed, whole_branch, 0, 0).astype(BF16)
    cut = BLOCK // 2
    places = tuple(range(6)) + tuple(range(8, 14)) + (6, 7, 14, 15)
    starts = tuple(place * cut for place in places)
    far = gather_far(begun)
    early = branch_step(mixed, right, gather_near(begun), starts[:12], (), False)
    far, early = tie(far, early)
    return branch_step(mixed, right, gather_late(far), starts[12:], early, True)


def turn_tables(blocks):
    prompt_blocks = blocks // 2
    later = CONT // BLOCK
    token = jnp.arange(blocks * BLOCK, dtype=jnp.int32)
    code = token // BLOCK
    inner = token % BLOCK
    place = jnp.where(
        code < prompt_blocks,
        token,
        prompt_blocks * BLOCK + (code - prompt_blocks) % later * BLOCK + inner,
    )
    half = ROTARY // 2
    freq = jnp.power(ROPE_BASE, -2.0 * jnp.arange(half, dtype=F32) / ROTARY)
    angle = place.astype(F32)[:, None] * freq[None, :]
    cosine, sine = jnp.cos(angle), jnp.sin(angle)
    rest = HEAD_DIM - ROTARY
    ones = jnp.ones((blocks * BLOCK, rest), F32)
    one_cos = jnp.concatenate([cosine, cosine, ones], axis=1)
    one_sin = jnp.concatenate([-sine, sine, 0.0 * ones], axis=1)
    return (jnp.tile(one_cos, (1, 2)), jnp.tile(one_sin, (1, 2)))


def local(
    layer_in,
    cotangent,
    block_map,
    attn_in,
    attn_out,
    ffn_in,
    ffn_out,
    vectors,
    first_attn_in,
    first_attn_out,
    first_ffn_in,
    first_ffn_out,
    first_vectors,
    second_attn_in,
    second_attn_out,
    second_ffn_in,
    second_ffn_out,
    second_vectors,
):
    cycle = lax.axis_size("ctx")
    groups = lax.axis_size("fsdp")
    here = lax.axis_index("ctx")
    owner = here * groups + lax.axis_index("fsdp")
    blocks = block_map.shape[1]
    rows = attn_in.shape[0]
    wide = D // cycle
    pairs = wide // LANES
    units = FF // cycle

    def rows_of(split):
        full = lax.all_gather(split, "fsdp", axis=0, tiled=False)
        return full.transpose(1, 0, 2, 3).reshape(D, split.shape[2])

    w_attn = lax.all_gather(attn_out.astype(BF16), "fsdp", axis=0, tiled=True)
    mine = vectors.astype(BF16).T.reshape(1, 7 * rows)
    below = jnp.pad(mine, ((0, 15), (0, 3 * wide - 7 * rows)))
    qkv_split = exchange(split_columns(attn_in, 3, below))
    w_qkv = rows_of(qkv_split[:, :rows])

    vec = qkv_split[:, rows, : 7 * rows].reshape(1, cycle, 7, rows)
    vec = lax.dynamic_update_slice(
        jnp.zeros((groups, cycle, 7, rows), BF16), vec, (lax.axis_index("fsdp"), 0, 0, 0)
    )
    vec = sum_everywhere(vec, ("fsdp",)).transpose(2, 1, 0, 3).reshape(7, D).astype(F32)

    x_pieces, vec, w_attn, ffn_in_late, cot_own = tie(
        gather_pieces(gather_start(*halves(layer_in[0]))), vec, w_attn, ffn_in, cotangent[0]
    )
    attn_act = norm_pieces(x_pieces, vec[0:1], vec[1:2])
    cot_begun = gather_start(*halves(cot_own))
    up_split, down_own, attn_act, first = tie(
        exchange(split_columns(ffn_in_late, 2)), ffn_out.astype(BF16), attn_act, cot_begun[4:6]
    )
    cot_begun = (*cot_begun[:4], *first, *cot_begun[6:])
    w_up = rows_of(up_split)
    w_down = lax.all_gather(down_own, "fsdp", axis=0, tiled=True)

    codes = block_map[0][places()]
    inv = jnp.argsort(codes).astype(jnp.int32)
    cosine, sine = turn_tables(blocks)
    bias = lax.dynamic_slice_in_dim(vec[2:5], here * wide, wide, 1).reshape(1, 3 * wide)
    project = dot(attn_act, w_qkv, 1, 0)
    project, cot_begun = tie(project, cot_begun)
    query, key, value, mixed, lse = attend(inv, project, bias, cosine, sine, pairs, blocks)
    cot_far = gather_far(cot_begun)
    mixed, cot_far = tie(mixed, cot_far)
    away = scatter_away(mixed, w_attn, 0)
    begun = scatter_start(scatter_sums(mixed, w_attn, 0, away))
    cot_low = jnp.concatenate(gather_pieces(cot_begun, cot_far), axis=0)
    begun, cot_low, w_up = window(begun, cot_low, w_up)
    parts = scatter_end(begun)
    resid, act_top, act_low = own_rows(enter_feed, layer_in[0], vec[5:6], vec[6:7], *parts)

    def owners(grad):
        return lax.psum_scatter(grad, "fsdp", scatter_dimension=0, tiled=True)

    def by_owner(grad):
        wider = grad.shape[1]
        return grad.reshape(-1, groups, rows, wider).transpose(1, 0, 2, 3).reshape(-1, wider)

    def owners_of_rows(grad):
        return owners(grad).reshape(-1, rows, grad.shape[1])

    ffn_act, both, hidden = ffn_up(gather_start(act_top, act_low), w_up, units)
    grad_both = ffn_back(both, cot_low, w_down, units)
    away = scatter_away(grad_both, w_up, 1)
    away, grad_down = tie(away, dot(hidden, cot_low, 0, 0).astype(BF16))
    share_down = owners(grad_down)
    begun = scatter_start(scatter_sums(grad_both, w_up, 1, away))
    grad_in = by_owner(dot(ffn_act, grad_both, 0, 0).astype(BF16))
    parts, grad_in = tie(scatter_end(begun), grad_in)
    share_in = owners_of_rows(grad_in)
    grad_resid, branch_top, branch_low, gain_two, shift_two = own_rows(
        leave_feed, cotangent[0], resid, vec[5:6], *parts
    )

    begun = gather_start(branch_top, branch_low)
    if cube():
        c_top, hidden = tie(begun[2], hidden)
        begun = (*begun[:2], c_top, *begun[3:])
    out_sums = scatter_sums(hidden, w_down, 0, scatter_away(hidden, w_down, 0))
    begun, out_sums = window(begun, out_sums)
    grad_mixed, grad_out = branch_grads(mixed, w_attn, begun)
    share_out = owners(grad_out)
    grad_mixed, out_sums, share_down = tie(grad_mixed, out_sums, share_down)
    out_begun = scatter_start(out_sums)
    grad_project = attend_back(
        inv, query, key, value, grad_mixed, lse, cosine, sine, pairs, blocks
    )
    grad_project, out_begun, share_in = tie(grad_project, out_begun, share_in)
    out_parts = scatter_end(out_begun)
    away = scatter_away(grad_project, w_qkv, 1)
    grad_qkv = by_owner(dot(attn_act, grad_project, 0, 0).astype(BF16))
    away, grad_qkv = tie(away, grad_qkv)
    share_qkv = owners_of_rows(grad_qkv)
    sums = scatter_sums(grad_project, w_qkv, 1, away)
    sums, share_in, share_out, grad_project = tie(sums, share_in, share_out, grad_project)
    begun = scatter_start(sums)
    begun, out_parts, split_in = window(begun, out_parts, exchange(share_in))
    layer_out = (resid + total_of(out_parts)).astype(BF16)[None]
    parts = scatter_end(begun)
    input_grad, gain_one, shift_one = own_rows(
        leave_layer, layer_in[0], grad_resid, vec[0:1], *parts
    )
    split_qkv = exchange(share_qkv)

    squares = F32(0.0)
    for share in (share_qkv, share_out, share_in, share_down):
        wide_share = share.astype(F32)
        squares = squares + jnp.sum(wide_share * wide_share)
    bias_grads = jnp.sum(grad_project.astype(F32), axis=0).reshape(3, wide)
    bias_grads = lax.dynamic_update_slice(jnp.zeros((3, D), F32), bias_grads, (0, here * wide))
    sums = jnp.concatenate(
        [
            gain_one,
            shift_one,
            bias_grads,
            gain_two,
            shift_two,
            jnp.where(jnp.arange(D)[None] == 0, squares, 0.0),
        ],
        axis=0,
    )
    sums, split_qkv = tie(sum_everywhere(sums, ("ctx",)), split_qkv)
    sums = sum_everywhere(sums, ("fsdp",))
    vector_sums = sums[:7]
    grad_norm = jnp.sqrt(jnp.sum(vector_sums * vector_sums) + sums[7, 0])
    mine = jnp.arange(D)[:, None] == owner * rows + jnp.arange(rows)[None]
    vector_grads = lax.dot_general(
        mine.astype(F32), vector_sums, (((0,), (1,)), ((), ())), precision=lax.Precision.HIGHEST
    )
    clip = jnp.minimum(1.0, CLIP_LIMIT / (grad_norm + 1e-06))
    grad_list = (
        join_columns(split_qkv, 3),
        share_out,
        join_columns(split_in, 2),
        share_down,
        vector_grads,
    )
    rates = (D ** (-0.5), 0.6 * max(D // 64, 32) ** (-0.5), D ** (-0.5), (FF // 4) ** (-0.5), 0.3)
    weights = (attn_in, attn_out, ffn_in, ffn_out, vectors)
    firsts = (first_attn_in, first_attn_out, first_ffn_in, first_ffn_out, first_vectors)
    seconds = (second_attn_in, second_attn_out, second_ffn_in, second_ffn_out, second_vectors)
    updated = []
    for index in range(5):
        updated.extend(
            adam(
                weights[index], clip * grad_list[index].astype(F32), firsts[index], seconds[index], rates[index]
            )
        )
    return (layer_out, input_grad[None], grad_norm, *updated)


def solution(mesh):
    tokens = P("fsdp", "ctx", None)
    owned = P(("ctx", "fsdp"), None)
    return jax.shard_map(
        local,
        mesh=mesh,
        in_specs=(tokens, tokens, P("fsdp", None)) + (owned,) * 15,
        out_specs=(tokens, tokens, P()) + (owned,) * 15,
        check_vma=False,
    )
```

```python
import functools
import math

import jax
import jax.numpy as jnp
from jax import lax
from jax.experimental import pallas as pl
from jax.experimental.pallas import tpu as pltpu
from jax.sharding import PartitionSpec as P

D = 2048
HEADS = 32
HEAD_DIM = 64
FF = 5632
ROTARY = 16
CONT = 1024
BLOCK = 256
STEP = 10

NORM_EPS = 1e-05
BETA_ONE = 0.9
BETA_TWO = 0.95
ADAM_EPS = 1e-08
DECAY = 0.1
CLIP_LIMIT = 1.0
ROPE_BASE = 10000.0
MASKED = -1e30
LANES = 128
SCALE = HEAD_DIM**-0.5
SCALE_LOG2 = SCALE * math.log2(math.e)
VMEM_LIMIT = 32 * 1024 * 1024
VMEM_MOST = 40 * 1024 * 1024
BF16 = jnp.bfloat16
SHORT = pl.CostEstimate(flops=1000000, bytes_accessed=1000000, transcendentals=0)
F32 = jnp.float32

ORDER = (0, 2, 4, 6, 1, 3, 5, 7)


def standardize(values):
    center = values - jnp.mean(values, axis=-1, keepdims=True)
    scaled = lax.rsqrt(jnp.mean(center * center, axis=-1, keepdims=True) + NORM_EPS)
    return (center * scaled, scaled)


def norm_back(grad_normed, normed, scaled):
    return scaled * (
        grad_normed
        - jnp.mean(grad_normed, axis=-1, keepdims=True)
        - normed * jnp.mean(grad_normed * normed, axis=-1, keepdims=True)
    )


def adam(weight, grad, first, second, rate):
    first = BETA_ONE * first + (1.0 - BETA_ONE) * grad
    second = BETA_TWO * second + (1.0 - BETA_TWO) * grad * grad
    fixed_first = first / (1.0 - BETA_ONE**STEP)
    fixed_second = second / (1.0 - BETA_TWO**STEP)
    weight = weight - rate * (fixed_first / (jnp.sqrt(fixed_second) + ADAM_EPS) + DECAY * weight)
    return (weight, first, second)


def dot(left, right, left_dim, right_dim):
    return lax.dot_general(
        left, right, (((left_dim,), (right_dim,)), ((), ())), preferred_element_type=F32
    )


def swap(value, bit, axis="ctx"):
    size = lax.axis_size(axis)
    return lax.ppermute(value, axis, [(i, i ^ bit) for i in range(size)])


def cube():
    return lax.axis_size("ctx") == 8


def places():
    size = lax.axis_size("ctx")
    if cube():
        return lax.axis_index("ctx") ^ jnp.array(ORDER, jnp.int32)
    return jnp.arange(size, dtype=jnp.int32)


def tie(*values):
    return lax.optimization_barrier(values)


def window(begun, *others):
    if not cube():
        return (begun, *others)
    tied = tie(*begun[-2:], *others)
    return (begun[:-2] + tied[:2], *tied[2:])


def gather_start(top, low, strict=False):
    if not cube():
        return (lax.all_gather(jnp.concatenate([top, low]), "ctx", axis=0, tiled=True),)
    x_top = swap(top, 2)
    y_low = swap(low, 4)
    c_top = swap(top, 1)
    c_low = swap(low, 1)
    if strict:
        x_top, y_low, top, low = tie(x_top, y_low, top, low)
    else:
        c_top, c_low, top, low = tie(c_top, c_low, top, low)
    return (top, low, c_top, c_low, x_top, y_low, swap(low, 2), swap(top, 4))


def gather_far(begun):
    if not cube():
        return ()
    return (swap(begun[4], 4), swap(begun[5], 2))


def gather_near(begun):
    top, low, c_top, c_low, x_top, y_low, x_low, y_top = begun
    near = (x_top, x_low, y_top, y_low)
    return (top, low, *near, c_top, c_low) + tuple(swap(piece, 1) for piece in near)


def gather_late(far):
    return far + tuple(swap(piece, 1) for piece in far)


def gather_pieces(begun, far=None):
    if not cube():
        return begun
    near = gather_near(begun)
    late = gather_late(gather_far(begun) if far is None else far)
    return near[:6] + late[:2] + near[6:] + late[2:]


def chip_kernel(right_dim, left_ref, right_ref, other_ref, own, x_top, x_low, y_top, y_low, d_top, d_low):
    total = dot(left_ref[...], right_ref[...], 1, right_dim) + other_ref[...].astype(F32)
    low = total.astype(BF16)
    half = BLOCK // 2

    @pl.when(pl.program_id(0) == 0)
    def _():
        own[...] = low[:BLOCK]
        x_top[...] = low[BLOCK : BLOCK + half]
        x_low[...] = low[BLOCK + half :]

    @pl.when(pl.program_id(0) == 1)
    def _():
        y_top[...] = low[:half]
        y_low[...] = low[half:BLOCK]
        d_top[...] = low[BLOCK : BLOCK + half]
        d_low[...] = low[BLOCK + half :]


def chip_sums(left, right, right_dim, other):
    depth = left.shape[1]
    half = BLOCK // 2
    cuts = (BLOCK,) + (half,) * 6
    return pl.pallas_call(
        functools.partial(chip_kernel, right_dim),
        grid=(2,),
        out_shape=tuple(jax.ShapeDtypeStruct((cut, D), BF16) for cut in cuts),
        in_specs=[
            pl.BlockSpec((2 * BLOCK, depth), lambda i: (i, 0)),
            pl.BlockSpec(right.shape, lambda i: (0, 0), pipeline_mode=pl.Buffered(1)),
            pl.BlockSpec((2 * BLOCK, D), lambda i: (i, 0)),
        ],
        out_specs=tuple(pl.BlockSpec((cut, D), lambda i: (0, 0)) for cut in cuts),
        compiler_params=pltpu.CompilerParams(vmem_limit_bytes=VMEM_LIMIT),
        cost_estimate=SHORT,
        name="chip_sums",
    )(left, right, other)


def scatter_away(left, right, right_dim):
    if not cube():
        return None
    return swap(dot(left[4 * BLOCK :], right, 1, right_dim).astype(BF16), 1)


def scatter_sums(left, right, right_dim, away):
    if not cube():
        part = dot(left, right, 1, right_dim).astype(BF16)
        return (lax.psum_scatter(part, "ctx", scatter_dimension=0, tiled=True),)
    return tuple(chip_sums(left, right, right_dim, away))


def scatter_start(sums, urgent=True):
    if not cube():
        return sums
    own, x_top, x_low, y_top, y_low, d_top, d_low = sums
    d_top, d_low = swap(d_top, 2), swap(d_low, 4)
    if urgent:
        d_top, d_low, x_top, y_low = tie(d_top, d_low, x_top, y_low)
    return (own, x_low, y_top, d_top, d_low, swap(x_top, 2), swap(y_low, 4))


def scatter_end(begun):
    if not cube():
        return begun
    own, x_low, y_top, d_top, d_low, x_top, y_low = begun
    x_low = swap((x_low.astype(F32) + d_low.astype(F32)).astype(BF16), 2)
    y_top = swap((y_top.astype(F32) + d_top.astype(F32)).astype(BF16), 4)
    return (own, x_top, y_top, x_low, y_low)


def total_of(parts):
    parts = [part.astype(F32) for part in parts]
    if len(parts) == 1:
        return parts[0]
    own, x_top, y_top, x_low, y_low = parts
    return own + jnp.concatenate([x_top + y_top, x_low + y_low], axis=0)


def split_kernel(parts, size, width, w_ref, *refs):
    rows = w_ref.shape[0]
    out_ref = refs[-1]
    for c in range(size):
        for p in range(parts):
            column = (p * size + c) * width
            block = w_ref[:, column : column + width].astype(BF16)
            out_ref[c, :rows, p * width : (p + 1) * width] = block
        if len(refs) > 1:
            out_ref[c, rows:, :] = refs[0][...]


def join_kernel(parts, size, width, share_ref, out_ref):
    for c in range(size):
        for p in range(parts):
            column = (p * size + c) * width
            out_ref[:, column : column + width] = share_ref[c, :, p * width : (p + 1) * width]


def relayout(kernel, values, shape, name):
    return pl.pallas_call(
        kernel,
        out_shape=jax.ShapeDtypeStruct(shape, BF16),
        in_specs=[pl.BlockSpec(memory_space=pltpu.VMEM)] * len(values),
        out_specs=pl.BlockSpec(memory_space=pltpu.VMEM),
        compiler_params=pltpu.CompilerParams(vmem_limit_bytes=VMEM_LIMIT),
        cost_estimate=SHORT,
        name=name,
    )(*values)


def split_columns(weight, parts, *below):
    size = lax.axis_size("ctx")
    rows = weight.shape[0]
    width = weight.shape[1] // (parts * size)
    if not cube():
        split = weight.astype(BF16).reshape(rows, parts, size, width)
        split = split.transpose(2, 0, 1, 3).reshape(size, rows, parts * width)
        below = [jnp.broadcast_to(value, (size, *value.shape)) for value in below]
        return jnp.concatenate([split, *below], axis=1)
    kernel = functools.partial(split_kernel, parts, size, width)
    total = rows + sum(value.shape[0] for value in below)
    return relayout(kernel, (weight, *below), (size, total, parts * width), "split_columns")


def join_columns(share, parts):
    size, rows, width = share.shape
    width = width // parts
    if not cube():
        split = share.reshape(size, rows, parts, width)
        return split.transpose(1, 2, 0, 3).reshape(rows, parts * size * width)
    kernel = functools.partial(join_kernel, parts, size, width)
    return relayout(kernel, (share,), (rows, parts * size * width), "join_columns")


def squared(share):
    share = share.astype(F32)
    return jnp.sum(share * share)


def exchange(split):
    return lax.all_to_all(split, "ctx", 0, 0)


def sum_everywhere(value, axes=("ctx", "fsdp")):
    for axis in axes:
        bit = 1
        while bit < lax.axis_size(axis):
            value = value + swap(value, bit, axis)
            bit *= 2
    return value


def aligned(index, step=BLOCK):
    return pl.ds(pl.multiple_of(index * step, step), step)


def span(start, count):
    return pl.ds(pl.multiple_of(start * BLOCK, BLOCK), count * BLOCK)


def over_blocks(full, step, state):
    for count in (4, 2, 1):
        start = full - lax.rem(full, 2 * count) if count < 4 else 0
        steps = lax.rem(full, 2 * count) // count if count < 4 else full // count
        state = lax.fori_loop(
            0,
            steps,
            lambda i, state, start=start, count=count: step(start + i * count, count, state),
            state,
        )
    return state


def turn(field, cosine, sine):
    lane = lax.broadcasted_iota(jnp.int32, field.shape, 1) % HEAD_DIM
    half = ROTARY // 2
    partner = jnp.where(
        lane < half, pltpu.roll(field, LANES - half, 1), pltpu.roll(field, half, 1)
    )
    return field * cosine + partner * sine


def full_blocks(code, prompt_blocks):
    later = CONT // BLOCK
    inside = lax.rem(code - prompt_blocks, later)
    return jnp.where(code < prompt_blocks, code, prompt_blocks + inside)


def key_block(code, index, prompt_blocks):
    later = CONT // BLOCK
    start = code - lax.rem(code - prompt_blocks, later)
    shifted = start + index - prompt_blocks
    return jnp.where(index < prompt_blocks, index, shifted)


def transposed(value):
    return value.astype(F32).T.astype(BF16)


def fold(value):
    return value.reshape(value.shape[0] // 8, 8, value.shape[1])


def split_rows(pair):
    zero = jnp.zeros((HEAD_DIM, pair.shape[1]), pair.dtype)
    return (
        jnp.concatenate([pair[:HEAD_DIM], zero], axis=0),
        jnp.concatenate([zero, pair[HEAD_DIM:]], axis=0),
    )


def causal():
    key = lax.broadcasted_iota(jnp.int32, (BLOCK, BLOCK), 0)
    query = lax.broadcasted_iota(jnp.int32, (BLOCK, BLOCK), 1)
    return key <= query


def attend_kernel(
    pairs, blocks, inv_ref, proj_ref, bias_ref, cos_ref, sin_ref, q_ref, k_ref, v_ref, mix_ref, lse_ref, vt_ref, s_ref
):
    prompt_blocks = blocks // 2
    wide = pairs * LANES
    lanes = [slice(p * LANES, (p + 1) * LANES) for p in range(pairs)]
    count = 2 * pairs

    def prepare(code, carry):
        rows = aligned(inv_ref[code])
        place = aligned(code)
        cosine = cos_ref[place, :]
        sine = sin_ref[place, :]
        for p in range(pairs):
            at = [slice(part * wide + p * LANES, part * wide + (p + 1) * LANES) for part in range(3)]
            field = [proj_ref[rows, a] + bias_ref[:, a] for a in at]
            q_ref[place, lanes[p]] = turn(field[0], cosine, sine).astype(BF16)
            k_ref[place, lanes[p]] = turn(field[1], cosine, sine).astype(BF16)
            v_ref[place, lanes[p]] = field[2].astype(BF16)
            vt_ref[lanes[p], place] = field[2].T.astype(BF16)
        return carry

    lax.fori_loop(0, blocks, prepare, 0)
    allowed = causal()

    def one_query(code, carry):
        place = aligned(code)
        rows = aligned(inv_ref[code])
        heads = []
        for p in range(pairs):
            heads.extend(split_rows(transposed(q_ref[place, lanes[p]])))

        def keys_at(index, number):
            return span(key_block(code, index, prompt_blocks), number)

        def scores(slot, at, mask, tops):
            fresh = []
            for h in range(count):
                logits = dot(k_ref[at, lanes[h // 2]], heads[h], 1, 0) * SCALE_LOG2
                if mask is not None:
                    logits = jnp.where(mask, logits, MASKED)
                s_ref[h, slot, :] = logits
                fresh.append(jnp.maximum(tops[h], jnp.max(fold(logits), axis=0)))
            return tuple(fresh)

        full = full_blocks(code, prompt_blocks)
        tops = scores(span(full, 1), place, allowed, (jnp.full((8, BLOCK), MASKED, F32),) * count)
        tops = over_blocks(
            full,
            lambda index, number, tops: scores(
                span(index, number), keys_at(index, number), None, tops
            ),
            tops,
        )
        tops = [jnp.max(top, axis=0, keepdims=True) for top in tops]

        def step(slot, at, state):
            fresh = []
            for h in range(count):
                total, mixed = state[h]
                probs = jnp.exp2(s_ref[h, slot, :] - tops[h])
                total = total + jnp.sum(fold(probs), axis=0)
                mixed = mixed + dot(
                    vt_ref[h * HEAD_DIM : (h + 1) * HEAD_DIM, at], probs.astype(BF16), 1, 0
                )
                fresh.append((total, mixed))
            return tuple(fresh)

        state = ((jnp.zeros((8, BLOCK), F32), jnp.zeros((HEAD_DIM, BLOCK), F32)),) * count
        state = step(span(full, 1), place, state)
        state = over_blocks(
            full,
            lambda index, number, state: step(
                span(index, number), keys_at(index, number), state
            ),
            state,
        )
        for p in range(pairs):
            both = []
            for h in (2 * p, 2 * p + 1):
                total, mixed = state[h]
                total = jnp.sum(total, axis=0, keepdims=True)
                both.append(mixed / total)
                lse_ref[h : h + 1, place] = tops[h] + jnp.log2(total)
            mix_ref[rows, lanes[p]] = jnp.concatenate(both, axis=0).T.astype(BF16)
        return carry

    lax.fori_loop(0, blocks, one_query, 0)


def attend(inv, project, bias, cosine, sine, pairs, blocks):
    tokens = blocks * BLOCK
    wide = pairs * LANES
    vmem = pl.BlockSpec(memory_space=pltpu.VMEM)
    low = jax.ShapeDtypeStruct((tokens, wide), BF16)
    return pl.pallas_call(
        functools.partial(attend_kernel, pairs, blocks),
        out_shape=(low, low, low, low, jax.ShapeDtypeStruct((2 * pairs, tokens), F32)),
        in_specs=[pl.BlockSpec(memory_space=pltpu.SMEM)] + [vmem] * 4,
        out_specs=(vmem,) * 5,
        scratch_shapes=[
            pltpu.VMEM((wide, tokens), BF16),
            pltpu.VMEM((2 * pairs, tokens, BLOCK), F32),
        ],
        compiler_params=pltpu.CompilerParams(vmem_limit_bytes=VMEM_LIMIT),
        cost_estimate=SHORT,
        name="attend",
    )(inv, project, bias, cosine, sine)


def attend_back_kernel(
    pairs, blocks, inv_ref, q_ref, k_ref, v_ref, do_ref, lse_ref, cos_ref, sin_ref, gp_ref, kt_ref, dk_ref, dv_ref, p_ref, dp_ref
):
    prompt_blocks = blocks // 2
    wide = pairs * LANES
    lanes = [slice(p * LANES, (p + 1) * LANES) for p in range(pairs)]
    count = 2 * pairs

    def prepare(code, carry):
        place = aligned(code)
        for p in range(pairs):
            kt_ref[lanes[p], place] = transposed(k_ref[place, lanes[p]])
            zero = jnp.zeros((BLOCK, LANES), F32)
            dk_ref[place, lanes[p]] = zero
            dv_ref[place, lanes[p]] = zero
        return carry

    lax.fori_loop(0, blocks, prepare, 0)
    allowed = causal()
    lane = lax.broadcasted_iota(jnp.int32, (BLOCK, LANES), 1)

    def one_query(code, carry):
        place = aligned(code)
        rows = aligned(inv_ref[code])
        q_heads, do_heads, q_rows, do_rows = [], [], [], []
        for p in range(pairs):
            query = q_ref[place, lanes[p]]
            grad = do_ref[rows, lanes[p]]
            q_heads.extend(split_rows(transposed(query)))
            do_heads.extend(split_rows(transposed(grad)))
            for h in range(2):
                mine = (lane >= h * HEAD_DIM) & (lane < (h + 1) * HEAD_DIM)
                q_rows.append(jnp.where(mine, query, jnp.zeros_like(query)))
                do_rows.append(jnp.where(mine, grad, jnp.zeros_like(grad)))

        def keys_at(index, number):
            return span(key_block(code, index, prompt_blocks), number)

        def probs_and_grads(slot, at, mask, sums):
            fresh = []
            for h in range(count):
                logits = dot(k_ref[at, lanes[h // 2]], q_heads[h], 1, 0) * SCALE_LOG2
                probs = jnp.exp2(logits - lse_ref[h : h + 1, place])
                if mask is not None:
                    probs = jnp.where(mask, probs, 0.0)
                grads = dot(v_ref[at, lanes[h // 2]], do_heads[h], 1, 0)
                p_ref[h, slot, :] = probs
                dp_ref[h, slot, :] = grads
                fresh.append(sums[h] + jnp.sum(fold(probs * grads), axis=0))
            return tuple(fresh)

        full = full_blocks(code, prompt_blocks)
        sums = (jnp.zeros((8, BLOCK), F32),) * count
        sums = probs_and_grads(span(full, 1), place, allowed, sums)
        sums = over_blocks(
            full,
            lambda index, number, sums: probs_and_grads(
                span(index, number), keys_at(index, number), None, sums
            ),
            sums,
        )
        sums = [jnp.sum(total, axis=0, keepdims=True) for total in sums]

        def step(slot, at, grads):
            fresh = []
            for p in range(pairs):
                for_key = dk_ref[at, lanes[p]]
                for_value = dv_ref[at, lanes[p]]
                for h in (2 * p, 2 * p + 1):
                    probs = p_ref[h, slot, :]
                    low = (probs * (dp_ref[h, slot, :] - sums[h])).astype(BF16)
                    for_key += dot(low, q_rows[h], 1, 0)
                    for_value += dot(probs.astype(BF16), do_rows[h], 1, 0)
                    fresh.append(
                        grads[h]
                        + dot(kt_ref[h * HEAD_DIM : (h + 1) * HEAD_DIM, at], low, 1, 0)
                    )
                dk_ref[at, lanes[p]] = for_key
                dv_ref[at, lanes[p]] = for_value
            return tuple(fresh)

        grads = step(span(full, 1), place, (jnp.zeros((HEAD_DIM, BLOCK), F32),) * count)
        grads = over_blocks(
            full,
            lambda index, number, grads: step(
                span(index, number), keys_at(index, number), grads
            ),
            grads,
        )
        for p in range(pairs):
            pair = jnp.concatenate([grads[2 * p], grads[2 * p + 1]], axis=0).T * SCALE
            gp_ref[rows, lanes[p]] = turn(pair, cos_ref[place, :], -sin_ref[place, :]).astype(BF16)
        return carry

    lax.fori_loop(0, blocks, one_query, 0)

    def finish(code, carry):
        place = aligned(code)
        rows = aligned(inv_ref[code])
        for p in range(pairs):
            pair = dk_ref[place, lanes[p]] * SCALE
            at = slice(wide + p * LANES, wide + (p + 1) * LANES)
            gp_ref[rows, at] = turn(pair, cos_ref[place, :], -sin_ref[place, :]).astype(BF16)
            at = slice(2 * wide + p * LANES, 2 * wide + (p + 1) * LANES)
            gp_ref[rows, at] = dv_ref[place, lanes[p]].astype(BF16)
        return carry

    lax.fori_loop(0, blocks, finish, 0)


def attend_back(inv, query, key, value, grad, lse, cosine, sine, pairs, blocks):
    tokens = blocks * BLOCK
    wide = pairs * LANES
    vmem = pl.BlockSpec(memory_space=pltpu.VMEM)
    return pl.pallas_call(
        functools.partial(attend_back_kernel, pairs, blocks),
        out_shape=jax.ShapeDtypeStruct((tokens, 3 * wide), BF16),
        in_specs=[pl.BlockSpec(memory_space=pltpu.SMEM)] + [vmem] * 7,
        out_specs=vmem,
        scratch_shapes=[
            pltpu.VMEM((wide, tokens), BF16),
            pltpu.VMEM((tokens, wide), F32),
            pltpu.VMEM((tokens, wide), F32),
            pltpu.VMEM((2 * pairs, tokens, BLOCK), F32),
            pltpu.VMEM((2 * pairs, tokens, BLOCK), F32),
        ],
        compiler_params=pltpu.CompilerParams(vmem_limit_bytes=VMEM_MOST),
        cost_estimate=SHORT,
        name="attend_back",
    )(inv, query, key, value, grad, lse, cosine, sine)


def load_tile(pieces, out_ref, tile):
    start = 0
    for piece in pieces:
        cut = piece.shape[0]

        @pl.when(pl.program_id(0) == start // tile)
        def _(piece=piece, start=start % tile, cut=cut):
            out_ref[start : start + cut, :] = piece[...]

        start += cut


def whole(value):
    return pl.BlockSpec(value.shape, lambda i: (0, 0), pipeline_mode=pl.Buffered(1))


def norm_kernel(gain_ref, shift_ref, *refs):
    out_ref, held = refs[-2:]
    load_tile(refs[:-2], held, BLOCK)
    normed, _ = standardize(held[...].astype(F32))
    out_ref[...] = (normed * gain_ref[...] + shift_ref[...]).astype(BF16)


def norm_pieces(pieces, gain, shift):
    if not cube():
        return (standardize(pieces[0].astype(F32))[0] * gain + shift).astype(BF16)
    tokens = sum(piece.shape[0] for piece in pieces)
    values = (gain, shift, *pieces)
    return pl.pallas_call(
        norm_kernel,
        grid=(tokens // BLOCK,),
        out_shape=jax.ShapeDtypeStruct((tokens, D), BF16),
        in_specs=[whole(value) for value in values],
        out_specs=pl.BlockSpec((BLOCK, D), lambda i: (i, 0)),
        scratch_shapes=[pltpu.VMEM((BLOCK, D), BF16)],
        compiler_params=pltpu.CompilerParams(vmem_limit_bytes=VMEM_LIMIT),
        cost_estimate=SHORT,
        name="norm_pieces",
    )(*values)


def halves(value):
    half = value.shape[0] // 2
    return value[:half], value[half:]


def enter_feed(inputs, gain, shift, *parts):
    resid = inputs.astype(F32) + total_of(parts)
    normed, _ = standardize(resid)
    return (resid, *halves((normed * gain + shift).astype(BF16)))


def leave_feed(cotangent, resid, gain, *parts):
    grad = total_of(parts)
    normed, scaled = standardize(resid)
    grad_resid = cotangent.astype(F32) + norm_back(grad * gain, normed, scaled)
    sums = [jnp.sum(grad * normed, axis=0, keepdims=True), jnp.sum(grad, axis=0, keepdims=True)]
    return (grad_resid, *halves(grad_resid.astype(BF16)), *sums)


def leave_layer(inputs, grad_resid, gain, *parts):
    grad = total_of(parts)
    normed, scaled = standardize(inputs.astype(F32))
    sums = [jnp.sum(grad * normed, axis=0, keepdims=True), jnp.sum(grad, axis=0, keepdims=True)]
    return (grad_resid + norm_back(grad * gain, normed, scaled), *sums)


def own_kernel(step, count, *refs):
    results = step(*(ref[...] for ref in refs[:count]))
    for ref, result in zip(refs[count:], results):
        ref[...] = result


def own_rows(step, *values):
    if not cube():
        return step(*values)
    vmem = pl.BlockSpec(memory_space=pltpu.VMEM)
    shapes = jax.eval_shape(step, *values)
    return pl.pallas_call(
        functools.partial(own_kernel, step, len(values)),
        out_shape=shapes,
        in_specs=[vmem] * len(values),
        out_specs=tuple(vmem for _ in shapes),
        compiler_params=pltpu.CompilerParams(vmem_limit_bytes=VMEM_LIMIT),
        cost_estimate=SHORT,
        name=step.__name__,
    )(*values)


def ffn_up_kernel(units, count, w_ref, *refs):
    act_ref, both_ref, hidden_ref = refs[-3:]
    load_tile(refs[:count], act_ref, BLOCK)
    both_ref[...] = dot(act_ref[...], w_ref[...], 1, 0)
    gate = both_ref[:, :units]
    upper = both_ref[:, units:]
    hidden_ref[...] = (gate * jax.nn.sigmoid(gate) * upper).astype(BF16)


def ffn_up_step(pieces, weight, units, place, before):
    steps = sum(piece.shape[0] for piece in pieces) // BLOCK
    tokens = lax.axis_size("ctx") * BLOCK
    count = len(pieces)
    return pl.pallas_call(
        functools.partial(ffn_up_kernel, units, count),
        grid=(steps,),
        out_shape=(
            jax.ShapeDtypeStruct((tokens, D), BF16),
            jax.ShapeDtypeStruct((tokens, 2 * units), F32),
            jax.ShapeDtypeStruct((tokens, units), BF16),
        ),
        in_specs=[whole(weight)]
        + [whole(piece) for piece in pieces]
        + [pl.BlockSpec(memory_space=pl.ANY)] * len(before),
        out_specs=(
            pl.BlockSpec((BLOCK, D), lambda i: (place(i), 0)),
            pl.BlockSpec((BLOCK, 2 * units), lambda i: (place(i), 0)),
            pl.BlockSpec((BLOCK, units), lambda i: (place(i), 0)),
        ),
        input_output_aliases={1 + count + k: k for k in range(len(before))},
        compiler_params=pltpu.CompilerParams(vmem_limit_bytes=VMEM_LIMIT),
        cost_estimate=SHORT,
        name="ffn_up",
    )(weight, *pieces, *before)


def ffn_up(begun, weight, units):
    if not cube():
        act = begun[0]
        both = dot(act, weight, 1, 0)
        gate = both[:, :units]
        return act, both, (gate * jax.nn.sigmoid(gate) * both[:, units:]).astype(BF16)
    far = gather_far(begun)
    early = ffn_up_step(gather_near(begun), weight, units, lambda i: i + i // 3, ())
    far, early = tie(far, early)
    return ffn_up_step(gather_late(far), weight, units, lambda i: 3 + 4 * i, early)


def ffn_back_kernel(units, both_ref, cot_ref, down_ref, gb_ref):
    grad = dot(cot_ref[...], down_ref[...], 1, 1)
    gate = both_ref[:, :units]
    upper = both_ref[:, units:]
    sigma = jax.nn.sigmoid(gate)
    gb_ref[:, :units] = (grad * upper * sigma * (1.0 + gate * (1.0 - sigma))).astype(BF16)
    gb_ref[:, units:] = (grad * (gate * sigma)).astype(BF16)


def ffn_back(both, cot, down, units):
    if not cube():
        grad = dot(cot, down, 1, 1)
        gate = both[:, :units]
        sigma = jax.nn.sigmoid(gate)
        grad_gate = grad * both[:, units:] * sigma * (1.0 + gate * (1.0 - sigma))
        return jnp.concatenate([grad_gate, grad * (gate * sigma)], axis=1).astype(BF16)
    tokens = cot.shape[0]
    tile = 2 * BLOCK
    return pl.pallas_call(
        functools.partial(ffn_back_kernel, units),
        grid=(tokens // tile,),
        out_shape=jax.ShapeDtypeStruct((tokens, 2 * units), BF16),
        in_specs=[
            pl.BlockSpec((tile, 2 * units), lambda i: (i, 0)),
            pl.BlockSpec((tile, D), lambda i: (i, 0)),
            pl.BlockSpec((units, D), lambda i: (0, 0), pipeline_mode=pl.Buffered(1)),
        ],
        out_specs=pl.BlockSpec((tile, 2 * units), lambda i: (i, 0)),
        compiler_params=pltpu.CompilerParams(vmem_limit_bytes=VMEM_LIMIT),
        cost_estimate=SHORT,
        name="ffn_back",
    )(both, cot, down)


def branch_kernel(first, last, starts, mixed_ref, right_ref, *refs):
    count = len(starts)
    left_ref, grad_ref = refs[-2:]
    total = jnp.zeros(grad_ref.shape, F32)
    if not first:
        left_ref[...] = refs[count][...]
        total = refs[count + 1][...]
    for start, ref in zip(starts, refs):
        stop = start + ref.shape[0]
        left_ref[start:stop, :] = dot(ref[...], right_ref[...], 1, 1).astype(BF16)
        total += dot(mixed_ref[start:stop, :], ref[...], 0, 0)
    grad_ref[...] = total.astype(grad_ref.dtype)


def branch_step(mixed, right, pieces, starts, before, last):
    vmem = pl.BlockSpec(memory_space=pltpu.VMEM)
    values = (mixed, right, *pieces, *before)
    return pl.pallas_call(
        functools.partial(branch_kernel, not before, last, starts),
        out_shape=(
            jax.ShapeDtypeStruct(mixed.shape, BF16),
            jax.ShapeDtypeStruct((mixed.shape[1], D), BF16 if last else F32),
        ),
        in_specs=[vmem] * len(values),
        out_specs=(vmem, vmem),
        compiler_params=pltpu.CompilerParams(vmem_limit_bytes=VMEM_LIMIT),
        cost_estimate=SHORT,
        name="branch_step",
    )(*values)


def branch_grads(mixed, right, begun):
    if not cube():
        (whole_branch,) = begun
        left = dot(whole_branch, right, 1, 1).astype(BF16)
        return left, dot(mixed, whole_branch, 0, 0).astype(BF16)
    cut = BLOCK // 2
    places = tuple(range(6)) + tuple(range(8, 14)) + (6, 7, 14, 15)
    starts = tuple(place * cut for place in places)
    far = gather_far(begun)
    early = branch_step(mixed, right, gather_near(begun), starts[:12], (), False)
    far, early = tie(far, early)
    return branch_step(mixed, right, gather_late(far), starts[12:], early, True)


def turn_tables(blocks):
    prompt_blocks = blocks // 2
    later = CONT // BLOCK
    token = jnp.arange(blocks * BLOCK, dtype=jnp.int32)
    code = token // BLOCK
    inner = token % BLOCK
    place = jnp.where(
        code < prompt_blocks,
        token,
        prompt_blocks * BLOCK + (code - prompt_blocks) % later * BLOCK + inner,
    )
    half = ROTARY // 2
    freq = jnp.power(ROPE_BASE, -2.0 * jnp.arange(half, dtype=F32) / ROTARY)
    angle = place.astype(F32)[:, None] * freq[None, :]
    cosine, sine = jnp.cos(angle), jnp.sin(angle)
    rest = HEAD_DIM - ROTARY
    ones = jnp.ones((blocks * BLOCK, rest), F32)
    one_cos = jnp.concatenate([cosine, cosine, ones], axis=1)
    one_sin = jnp.concatenate([-sine, sine, 0.0 * ones], axis=1)
    return (jnp.tile(one_cos, (1, 2)), jnp.tile(one_sin, (1, 2)))


def local(
    layer_in,
    cotangent,
    block_map,
    attn_in,
    attn_out,
    ffn_in,
    ffn_out,
    vectors,
    first_attn_in,
    first_attn_out,
    first_ffn_in,
    first_ffn_out,
    first_vectors,
    second_attn_in,
    second_attn_out,
    second_ffn_in,
    second_ffn_out,
    second_vectors,
):
    cycle = lax.axis_size("ctx")
    groups = lax.axis_size("fsdp")
    here = lax.axis_index("ctx")
    owner = here * groups + lax.axis_index("fsdp")
    blocks = block_map.shape[1]
    rows = attn_in.shape[0]
    wide = D // cycle
    pairs = wide // LANES
    units = FF // cycle

    def rows_of(split):
        full = lax.all_gather(split, "fsdp", axis=0, tiled=False)
        return full.transpose(1, 0, 2, 3).reshape(D, split.shape[2])

    w_attn = lax.all_gather(attn_out.astype(BF16), "fsdp", axis=0, tiled=True)
    mine = vectors.astype(BF16).T.reshape(1, 7 * rows)
    below = jnp.pad(mine, ((0, 15), (0, 3 * wide - 7 * rows)))
    qkv_split = exchange(split_columns(attn_in, 3, below))
    w_qkv = rows_of(qkv_split[:, :rows])

    vec = qkv_split[:, rows, : 7 * rows].reshape(1, cycle, 7, rows)
    vec = lax.dynamic_update_slice(
        jnp.zeros((groups, cycle, 7, rows), BF16), vec, (lax.axis_index("fsdp"), 0, 0, 0)
    )
    vec = sum_everywhere(vec, ("fsdp",)).transpose(2, 1, 0, 3).reshape(7, D).astype(F32)

    inv = jnp.argsort(block_map[0][places()]).astype(jnp.int32)
    x_pieces, vec, w_attn, ffn_in_late, cot_own, inv, cosine, sine = tie(
        gather_pieces(gather_start(*halves(layer_in[0]))),
        vec,
        w_attn,
        ffn_in,
        cotangent[0],
        inv,
        *turn_tables(blocks),
    )
    attn_act = norm_pieces(x_pieces, vec[0:1], vec[1:2])
    up_split, down_own, attn_act = tie(
        exchange(split_columns(ffn_in_late, 2)), ffn_out.astype(BF16), attn_act
    )
    w_up = rows_of(up_split)
    w_down = lax.all_gather(down_own, "fsdp", axis=0, tiled=True)

    bias = lax.dynamic_slice_in_dim(vec[2:5], here * wide, wide, 1).reshape(1, 3 * wide)
    project = dot(attn_act, w_qkv, 1, 0)
    project, cot_begun = tie(project, gather_start(*halves(cot_own)))
    query, key, value, mixed, lse = attend(inv, project, bias, cosine, sine, pairs, blocks)
    cot_far = gather_far(cot_begun)
    mixed, cot_far = tie(mixed, cot_far)
    away = scatter_away(mixed, w_attn, 0)
    begun = scatter_start(scatter_sums(mixed, w_attn, 0, away))
    cot_low = jnp.concatenate(gather_pieces(cot_begun, cot_far), axis=0)
    begun, cot_low, w_up = window(begun, cot_low, w_up)
    parts = scatter_end(begun)
    resid, act_top, act_low = own_rows(enter_feed, layer_in[0], vec[5:6], vec[6:7], *parts)

    def owners(grad):
        return lax.psum_scatter(grad, "fsdp", scatter_dimension=0, tiled=True)

    def by_owner(grad):
        wider = grad.shape[1]
        return grad.reshape(-1, groups, rows, wider).transpose(1, 0, 2, 3).reshape(-1, wider)

    def owners_of_rows(grad):
        return owners(grad).reshape(-1, rows, grad.shape[1])

    ffn_act, both, hidden = ffn_up(gather_start(act_top, act_low), w_up, units)
    grad_both = ffn_back(both, cot_low, w_down, units)
    away = scatter_away(grad_both, w_up, 1)
    away, grad_down = tie(away, dot(hidden, cot_low, 0, 0).astype(BF16))
    share_down = owners(grad_down)
    begun = scatter_start(scatter_sums(grad_both, w_up, 1, away))
    grad_in = by_owner(dot(ffn_act, grad_both, 0, 0).astype(BF16))
    parts, grad_in = tie(scatter_end(begun), grad_in)
    share_in = owners_of_rows(grad_in)
    grad_resid, branch_top, branch_low, gain_two, shift_two = own_rows(
        leave_feed, cotangent[0], resid, vec[5:6], *parts
    )

    begun = gather_start(branch_top, branch_low, True)
    if cube():
        c_top, hidden = tie(begun[2], hidden)
        begun = (*begun[:2], c_top, *begun[3:])
    out_sums = scatter_sums(hidden, w_down, 0, scatter_away(hidden, w_down, 0))
    begun, out_sums = window(begun, out_sums)
    grad_mixed, grad_out = branch_grads(mixed, w_attn, begun)
    share_out = owners(grad_out)
    grad_mixed, out_sums, share_down = tie(grad_mixed, out_sums, share_down)
    out_begun = scatter_start(out_sums, False)
    grad_project = attend_back(
        inv, query, key, value, grad_mixed, lse, cosine, sine, pairs, blocks
    )
    grad_project, out_begun, share_in = tie(grad_project, out_begun, share_in)
    out_parts = scatter_end(out_begun)
    away = scatter_away(grad_project, w_qkv, 1)
    grad_qkv = by_owner(dot(attn_act, grad_project, 0, 0).astype(BF16))
    away, grad_qkv = tie(away, grad_qkv)
    share_qkv = owners_of_rows(grad_qkv)
    sums = scatter_sums(grad_project, w_qkv, 1, away)
    sums, grad_project, out_parts, share_in, share_out, share_down = tie(
        sums, grad_project, out_parts, share_in, share_out, share_down
    )
    layer_out = (resid + total_of(out_parts)).astype(BF16)[None]
    bias_grads = jnp.sum(grad_project.astype(F32), axis=0).reshape(3, wide)
    bias_grads = lax.dynamic_update_slice(jnp.zeros((3, D), F32), bias_grads, (0, here * wide))
    squares = squared(share_in) + squared(share_out) + squared(share_down)
    parts, layer_out, bias_grads, squares, share_in = tie(
        scatter_end(scatter_start(sums)), layer_out, bias_grads, squares, share_in
    )
    split_in = exchange(share_in)
    input_grad, gain_one, shift_one = own_rows(
        leave_layer, layer_in[0], grad_resid, vec[0:1], *parts
    )
    gain_one, shift_one, share_qkv = tie(gain_one, shift_one, share_qkv)
    split_qkv = exchange(share_qkv)

    squares = squares + squared(share_qkv)
    sums = jnp.concatenate(
        [
            gain_one,
            shift_one,
            bias_grads,
            gain_two,
            shift_two,
            jnp.where(jnp.arange(D)[None] == 0, squares, 0.0),
        ],
        axis=0,
    )
    sums = sum_everywhere(sums)
    vector_sums = sums[:7]
    grad_norm = jnp.sqrt(jnp.sum(vector_sums * vector_sums) + sums[7, 0])
    mine = jnp.arange(D)[:, None] == owner * rows + jnp.arange(rows)[None]
    vector_grads = lax.dot_general(
        mine.astype(F32), vector_sums, (((0,), (1,)), ((), ())), precision=lax.Precision.HIGHEST
    )
    clip = jnp.minimum(1.0, CLIP_LIMIT / (grad_norm + 1e-06))
    grad_list = (
        join_columns(split_qkv, 3),
        share_out,
        join_columns(split_in, 2),
        share_down,
        vector_grads,
    )
    rates = (D ** (-0.5), 0.6 * max(D // 64, 32) ** (-0.5), D ** (-0.5), (FF // 4) ** (-0.5), 0.3)
    weights = (attn_in, attn_out, ffn_in, ffn_out, vectors)
    firsts = (first_attn_in, first_attn_out, first_ffn_in, first_ffn_out, first_vectors)
    seconds = (second_attn_in, second_attn_out, second_ffn_in, second_ffn_out, second_vectors)
    updated = []
    for index in range(5):
        updated.extend(
            adam(
                weights[index], clip * grad_list[index].astype(F32), firsts[index], seconds[index], rates[index]
            )
        )
    return (layer_out, input_grad[None], grad_norm, *updated)


def solution(mesh):
    tokens = P("fsdp", "ctx", None)
    owned = P(("ctx", "fsdp"), None)
    return jax.shard_map(
        local,
        mesh=mesh,
        in_specs=(tokens, tokens, P("fsdp", None)) + (owned,) * 15,
        out_specs=(tokens, tokens, P()) + (owned,) * 15,
        check_vma=False,
    )
```

```python
import functools
import math

import jax
import jax.numpy as jnp
from jax import lax
from jax.experimental import pallas as pl
from jax.experimental.pallas import tpu as pltpu
from jax.sharding import PartitionSpec as P

D = 2048
HEADS = 32
HEAD_DIM = 64
FF = 5632
ROTARY = 16
CONT = 1024
BLOCK = 256
STEP = 10

NORM_EPS = 1e-05
BETA_ONE = 0.9
BETA_TWO = 0.95
ADAM_EPS = 1e-08
DECAY = 0.1
CLIP_LIMIT = 1.0
ROPE_BASE = 10000.0
MASKED = -1e30
LANES = 128
SCALE = HEAD_DIM**-0.5
SCALE_LOG2 = SCALE * math.log2(math.e)
VMEM_LIMIT = 32 * 1024 * 1024
VMEM_MOST = 40 * 1024 * 1024
BF16 = jnp.bfloat16
SHORT = pl.CostEstimate(flops=1000000, bytes_accessed=1000000, transcendentals=0)
F32 = jnp.float32

ORDER = (0, 2, 4, 6, 1, 3, 5, 7)


def standardize(values):
    center = values - jnp.mean(values, axis=-1, keepdims=True)
    scaled = lax.rsqrt(jnp.mean(center * center, axis=-1, keepdims=True) + NORM_EPS)
    return (center * scaled, scaled)


def norm_back(grad_normed, normed, scaled):
    return scaled * (
        grad_normed
        - jnp.mean(grad_normed, axis=-1, keepdims=True)
        - normed * jnp.mean(grad_normed * normed, axis=-1, keepdims=True)
    )


def adam(weight, grad, first, second, rate):
    first = BETA_ONE * first + (1.0 - BETA_ONE) * grad
    second = BETA_TWO * second + (1.0 - BETA_TWO) * grad * grad
    fixed_first = first / (1.0 - BETA_ONE**STEP)
    fixed_second = second / (1.0 - BETA_TWO**STEP)
    weight = weight - rate * (fixed_first / (jnp.sqrt(fixed_second) + ADAM_EPS) + DECAY * weight)
    return (weight, first, second)


def dot(left, right, left_dim, right_dim):
    return lax.dot_general(
        left, right, (((left_dim,), (right_dim,)), ((), ())), preferred_element_type=F32
    )


def swap(value, bit, axis="ctx"):
    size = lax.axis_size(axis)
    return lax.ppermute(value, axis, [(i, i ^ bit) for i in range(size)])


def cube():
    return lax.axis_size("ctx") == 8


def places():
    size = lax.axis_size("ctx")
    if cube():
        return lax.axis_index("ctx") ^ jnp.array(ORDER, jnp.int32)
    return jnp.arange(size, dtype=jnp.int32)


def tie(*values):
    return lax.optimization_barrier(values)


def window(begun, *others):
    if not cube():
        return (begun, *others)
    tied = tie(*begun[-2:], *others)
    return (begun[:-2] + tied[:2], *tied[2:])


def gather_start(top, low, strict=False):
    if not cube():
        return (lax.all_gather(jnp.concatenate([top, low]), "ctx", axis=0, tiled=True),)
    x_top = swap(top, 2)
    y_low = swap(low, 4)
    c_top = swap(top, 1)
    c_low = swap(low, 1)
    if strict:
        x_top, y_low, top, low = tie(x_top, y_low, top, low)
    else:
        c_top, c_low, top, low = tie(c_top, c_low, top, low)
    return (top, low, c_top, c_low, x_top, y_low, swap(low, 2), swap(top, 4))


def gather_far(begun):
    if not cube():
        return ()
    return (swap(begun[4], 4), swap(begun[5], 2))


def gather_near(begun):
    top, low, c_top, c_low, x_top, y_low, x_low, y_top = begun
    near = (x_top, x_low, y_top, y_low)
    return (top, low, *near, c_top, c_low) + tuple(swap(piece, 1) for piece in near)


def gather_late(far):
    return far + tuple(swap(piece, 1) for piece in far)


def gather_pieces(begun, far=None):
    if not cube():
        return begun
    near = gather_near(begun)
    late = gather_late(gather_far(begun) if far is None else far)
    return near[:6] + late[:2] + near[6:] + late[2:]


def chip_kernel(right_dim, left_ref, right_ref, other_ref, own, x_top, x_low, y_top, y_low, d_top, d_low):
    total = dot(left_ref[...], right_ref[...], 1, right_dim) + other_ref[...].astype(F32)
    low = total.astype(BF16)
    half = BLOCK // 2

    @pl.when(pl.program_id(0) == 0)
    def _():
        own[...] = low[:BLOCK]
        x_top[...] = low[BLOCK : BLOCK + half]
        x_low[...] = low[BLOCK + half :]

    @pl.when(pl.program_id(0) == 1)
    def _():
        y_top[...] = low[:half]
        y_low[...] = low[half:BLOCK]
        d_top[...] = low[BLOCK : BLOCK + half]
        d_low[...] = low[BLOCK + half :]


def chip_sums(left, right, right_dim, other):
    depth = left.shape[1]
    half = BLOCK // 2
    cuts = (BLOCK,) + (half,) * 6
    return pl.pallas_call(
        functools.partial(chip_kernel, right_dim),
        grid=(2,),
        out_shape=tuple(jax.ShapeDtypeStruct((cut, D), BF16) for cut in cuts),
        in_specs=[
            pl.BlockSpec((2 * BLOCK, depth), lambda i: (i, 0)),
            pl.BlockSpec(right.shape, lambda i: (0, 0), pipeline_mode=pl.Buffered(1)),
            pl.BlockSpec((2 * BLOCK, D), lambda i: (i, 0)),
        ],
        out_specs=tuple(pl.BlockSpec((cut, D), lambda i: (0, 0)) for cut in cuts),
        compiler_params=pltpu.CompilerParams(vmem_limit_bytes=VMEM_LIMIT),
        cost_estimate=SHORT,
        name="chip_sums",
    )(left, right, other)


def scatter_away(left, right, right_dim):
    if not cube():
        return None
    return swap(dot(left[4 * BLOCK :], right, 1, right_dim).astype(BF16), 1)


def scatter_sums(left, right, right_dim, away):
    if not cube():
        part = dot(left, right, 1, right_dim).astype(BF16)
        return (lax.psum_scatter(part, "ctx", scatter_dimension=0, tiled=True),)
    return tuple(chip_sums(left, right, right_dim, away))


def scatter_start(sums, urgent=True):
    if not cube():
        return sums
    own, x_top, x_low, y_top, y_low, d_top, d_low = sums
    d_top, d_low = swap(d_top, 2), swap(d_low, 4)
    if urgent:
        d_top, d_low, x_top, y_low = tie(d_top, d_low, x_top, y_low)
    return (own, x_low, y_top, d_top, d_low, swap(x_top, 2), swap(y_low, 4))


def scatter_end(begun):
    if not cube():
        return begun
    own, x_low, y_top, d_top, d_low, x_top, y_low = begun
    x_low = swap((x_low.astype(F32) + d_low.astype(F32)).astype(BF16), 2)
    y_top = swap((y_top.astype(F32) + d_top.astype(F32)).astype(BF16), 4)
    return (own, x_top, y_top, x_low, y_low)


def total_of(parts):
    parts = [part.astype(F32) for part in parts]
    if len(parts) == 1:
        return parts[0]
    own, x_top, y_top, x_low, y_low = parts
    return own + jnp.concatenate([x_top + y_top, x_low + y_low], axis=0)


def split_kernel(parts, size, width, w_ref, *refs):
    rows = w_ref.shape[0]
    out_ref = refs[-1]
    for c in range(size):
        for p in range(parts):
            column = (p * size + c) * width
            block = w_ref[:, column : column + width].astype(BF16)
            out_ref[c, :rows, p * width : (p + 1) * width] = block
        if len(refs) > 1:
            out_ref[c, rows:, :] = refs[0][...]


def join_kernel(parts, size, width, share_ref, out_ref):
    for c in range(size):
        for p in range(parts):
            column = (p * size + c) * width
            out_ref[:, column : column + width] = share_ref[c, :, p * width : (p + 1) * width]


def relayout(kernel, values, shape, name):
    return pl.pallas_call(
        kernel,
        out_shape=jax.ShapeDtypeStruct(shape, BF16),
        in_specs=[pl.BlockSpec(memory_space=pltpu.VMEM)] * len(values),
        out_specs=pl.BlockSpec(memory_space=pltpu.VMEM),
        compiler_params=pltpu.CompilerParams(vmem_limit_bytes=VMEM_LIMIT),
        cost_estimate=SHORT,
        name=name,
    )(*values)


def split_columns(weight, parts, *below):
    size = lax.axis_size("ctx")
    rows = weight.shape[0]
    width = weight.shape[1] // (parts * size)
    if not cube():
        split = weight.astype(BF16).reshape(rows, parts, size, width)
        split = split.transpose(2, 0, 1, 3).reshape(size, rows, parts * width)
        below = [jnp.broadcast_to(value, (size, *value.shape)) for value in below]
        return jnp.concatenate([split, *below], axis=1)
    kernel = functools.partial(split_kernel, parts, size, width)
    total = rows + sum(value.shape[0] for value in below)
    return relayout(kernel, (weight, *below), (size, total, parts * width), "split_columns")


def join_columns(share, parts):
    size, rows, width = share.shape
    width = width // parts
    if not cube():
        split = share.reshape(size, rows, parts, width)
        return split.transpose(1, 2, 0, 3).reshape(rows, parts * size * width)
    kernel = functools.partial(join_kernel, parts, size, width)
    return relayout(kernel, (share,), (rows, parts * size * width), "join_columns")


def squared(share):
    share = share.astype(F32)
    return jnp.sum(share * share)


def exchange(split):
    return lax.all_to_all(split, "ctx", 0, 0)


def sum_everywhere(value, axes=("ctx", "fsdp")):
    for axis in axes:
        bit = 1
        while bit < lax.axis_size(axis):
            value = value + swap(value, bit, axis)
            bit *= 2
    return value


def aligned(index, step=BLOCK):
    return pl.ds(pl.multiple_of(index * step, step), step)


def span(start, count):
    return pl.ds(pl.multiple_of(start * BLOCK, BLOCK), count * BLOCK)


def over_blocks(full, step, state):
    for count in (4, 2, 1):
        start = full - lax.rem(full, 2 * count) if count < 4 else 0
        steps = lax.rem(full, 2 * count) // count if count < 4 else full // count
        state = lax.fori_loop(
            0,
            steps,
            lambda i, state, start=start, count=count: step(start + i * count, count, state),
            state,
        )
    return state


def turn(field, cosine, sine):
    lane = lax.broadcasted_iota(jnp.int32, field.shape, 1) % HEAD_DIM
    half = ROTARY // 2
    partner = jnp.where(
        lane < half, pltpu.roll(field, LANES - half, 1), pltpu.roll(field, half, 1)
    )
    return field * cosine + partner * sine


def full_blocks(code, prompt_blocks):
    later = CONT // BLOCK
    inside = lax.rem(code - prompt_blocks, later)
    return jnp.where(code < prompt_blocks, code, prompt_blocks + inside)


def key_block(code, index, prompt_blocks):
    later = CONT // BLOCK
    start = code - lax.rem(code - prompt_blocks, later)
    shifted = start + index - prompt_blocks
    return jnp.where(index < prompt_blocks, index, shifted)


def transposed(value):
    return value.astype(F32).T.astype(BF16)


def fold(value):
    return value.reshape(value.shape[0] // 8, 8, value.shape[1])


def split_rows(pair):
    zero = jnp.zeros((HEAD_DIM, pair.shape[1]), pair.dtype)
    return (
        jnp.concatenate([pair[:HEAD_DIM], zero], axis=0),
        jnp.concatenate([zero, pair[HEAD_DIM:]], axis=0),
    )


def causal():
    key = lax.broadcasted_iota(jnp.int32, (BLOCK, BLOCK), 0)
    query = lax.broadcasted_iota(jnp.int32, (BLOCK, BLOCK), 1)
    return key <= query


def attend_kernel(
    pairs, blocks, inv_ref, proj_ref, bias_ref, cos_ref, sin_ref, q_ref, k_ref, v_ref, mix_ref, lse_ref, vt_ref, s_ref
):
    prompt_blocks = blocks // 2
    wide = pairs * LANES
    lanes = [slice(p * LANES, (p + 1) * LANES) for p in range(pairs)]
    count = 2 * pairs

    def prepare(code, carry):
        rows = aligned(inv_ref[code])
        place = aligned(code)
        cosine = cos_ref[place, :]
        sine = sin_ref[place, :]
        for p in range(pairs):
            at = [slice(part * wide + p * LANES, part * wide + (p + 1) * LANES) for part in range(3)]
            field = [proj_ref[rows, a] + bias_ref[:, a] for a in at]
            q_ref[place, lanes[p]] = turn(field[0], cosine, sine).astype(BF16)
            k_ref[place, lanes[p]] = turn(field[1], cosine, sine).astype(BF16)
            v_ref[place, lanes[p]] = field[2].astype(BF16)
            vt_ref[lanes[p], place] = field[2].T.astype(BF16)
        return carry

    lax.fori_loop(0, blocks, prepare, 0)
    allowed = causal()

    def one_query(code, carry):
        place = aligned(code)
        rows = aligned(inv_ref[code])
        heads = []
        for p in range(pairs):
            heads.extend(split_rows(transposed(q_ref[place, lanes[p]])))

        def keys_at(index, number):
            return span(key_block(code, index, prompt_blocks), number)

        def scores(slot, at, mask, tops):
            fresh = []
            for h in range(count):
                logits = dot(k_ref[at, lanes[h // 2]], heads[h], 1, 0) * SCALE_LOG2
                if mask is not None:
                    logits = jnp.where(mask, logits, MASKED)
                s_ref[h, slot, :] = logits
                fresh.append(jnp.maximum(tops[h], jnp.max(fold(logits), axis=0)))
            return tuple(fresh)

        full = full_blocks(code, prompt_blocks)
        tops = scores(span(full, 1), place, allowed, (jnp.full((8, BLOCK), MASKED, F32),) * count)
        tops = over_blocks(
            full,
            lambda index, number, tops: scores(
                span(index, number), keys_at(index, number), None, tops
            ),
            tops,
        )
        tops = [jnp.max(top, axis=0, keepdims=True) for top in tops]

        def step(slot, at, state):
            fresh = []
            for h in range(count):
                total, mixed = state[h]
                probs = jnp.exp2(s_ref[h, slot, :] - tops[h])
                total = total + jnp.sum(fold(probs), axis=0)
                mixed = mixed + dot(
                    vt_ref[h * HEAD_DIM : (h + 1) * HEAD_DIM, at], probs.astype(BF16), 1, 0
                )
                fresh.append((total, mixed))
            return tuple(fresh)

        state = ((jnp.zeros((8, BLOCK), F32), jnp.zeros((HEAD_DIM, BLOCK), F32)),) * count
        state = step(span(full, 1), place, state)
        state = over_blocks(
            full,
            lambda index, number, state: step(
                span(index, number), keys_at(index, number), state
            ),
            state,
        )
        for p in range(pairs):
            both = []
            for h in (2 * p, 2 * p + 1):
                total, mixed = state[h]
                total = jnp.sum(total, axis=0, keepdims=True)
                both.append(mixed / total)
                lse_ref[h : h + 1, place] = tops[h] + jnp.log2(total)
            mix_ref[rows, lanes[p]] = jnp.concatenate(both, axis=0).T.astype(BF16)
        return carry

    lax.fori_loop(0, blocks, one_query, 0)


def attend(inv, project, bias, cosine, sine, pairs, blocks):
    tokens = blocks * BLOCK
    wide = pairs * LANES
    vmem = pl.BlockSpec(memory_space=pltpu.VMEM)
    low = jax.ShapeDtypeStruct((tokens, wide), BF16)
    return pl.pallas_call(
        functools.partial(attend_kernel, pairs, blocks),
        out_shape=(low, low, low, low, jax.ShapeDtypeStruct((2 * pairs, tokens), F32)),
        in_specs=[pl.BlockSpec(memory_space=pltpu.SMEM)] + [vmem] * 4,
        out_specs=(vmem,) * 5,
        scratch_shapes=[
            pltpu.VMEM((wide, tokens), BF16),
            pltpu.VMEM((2 * pairs, tokens, BLOCK), F32),
        ],
        compiler_params=pltpu.CompilerParams(vmem_limit_bytes=VMEM_LIMIT),
        cost_estimate=SHORT,
        name="attend",
    )(inv, project, bias, cosine, sine)


def attend_back_kernel(
    pairs, blocks, inv_ref, q_ref, k_ref, v_ref, do_ref, lse_ref, cos_ref, sin_ref, gp_ref, kt_ref, dk_ref, dv_ref, p_ref, dp_ref
):
    prompt_blocks = blocks // 2
    wide = pairs * LANES
    lanes = [slice(p * LANES, (p + 1) * LANES) for p in range(pairs)]
    count = 2 * pairs

    def prepare(code, carry):
        place = aligned(code)
        for p in range(pairs):
            kt_ref[lanes[p], place] = transposed(k_ref[place, lanes[p]])
            zero = jnp.zeros((BLOCK, LANES), F32)
            dk_ref[place, lanes[p]] = zero
            dv_ref[place, lanes[p]] = zero
        return carry

    lax.fori_loop(0, blocks, prepare, 0)
    allowed = causal()
    lane = lax.broadcasted_iota(jnp.int32, (BLOCK, LANES), 1)

    def one_query(code, carry):
        place = aligned(code)
        rows = aligned(inv_ref[code])
        q_heads, do_heads, q_rows, do_rows = [], [], [], []
        for p in range(pairs):
            query = q_ref[place, lanes[p]]
            grad = do_ref[rows, lanes[p]]
            q_heads.extend(split_rows(transposed(query)))
            do_heads.extend(split_rows(transposed(grad)))
            for h in range(2):
                mine = (lane >= h * HEAD_DIM) & (lane < (h + 1) * HEAD_DIM)
                q_rows.append(jnp.where(mine, query, jnp.zeros_like(query)))
                do_rows.append(jnp.where(mine, grad, jnp.zeros_like(grad)))

        def keys_at(index, number):
            return span(key_block(code, index, prompt_blocks), number)

        def probs_and_grads(slot, at, mask, sums):
            fresh = []
            for h in range(count):
                logits = dot(k_ref[at, lanes[h // 2]], q_heads[h], 1, 0) * SCALE_LOG2
                probs = jnp.exp2(logits - lse_ref[h : h + 1, place])
                if mask is not None:
                    probs = jnp.where(mask, probs, 0.0)
                grads = dot(v_ref[at, lanes[h // 2]], do_heads[h], 1, 0)
                p_ref[h, slot, :] = probs
                dp_ref[h, slot, :] = grads
                fresh.append(sums[h] + jnp.sum(fold(probs * grads), axis=0))
            return tuple(fresh)

        full = full_blocks(code, prompt_blocks)
        sums = (jnp.zeros((8, BLOCK), F32),) * count
        sums = probs_and_grads(span(full, 1), place, allowed, sums)
        sums = over_blocks(
            full,
            lambda index, number, sums: probs_and_grads(
                span(index, number), keys_at(index, number), None, sums
            ),
            sums,
        )
        sums = [jnp.sum(total, axis=0, keepdims=True) for total in sums]

        def step(slot, at, grads):
            fresh = []
            for p in range(pairs):
                for_key = dk_ref[at, lanes[p]]
                for_value = dv_ref[at, lanes[p]]
                for h in (2 * p, 2 * p + 1):
                    probs = p_ref[h, slot, :]
                    low = (probs * (dp_ref[h, slot, :] - sums[h])).astype(BF16)
                    for_key += dot(low, q_rows[h], 1, 0)
                    for_value += dot(probs.astype(BF16), do_rows[h], 1, 0)
                    fresh.append(
                        grads[h]
                        + dot(kt_ref[h * HEAD_DIM : (h + 1) * HEAD_DIM, at], low, 1, 0)
                    )
                dk_ref[at, lanes[p]] = for_key
                dv_ref[at, lanes[p]] = for_value
            return tuple(fresh)

        grads = step(span(full, 1), place, (jnp.zeros((HEAD_DIM, BLOCK), F32),) * count)
        grads = over_blocks(
            full,
            lambda index, number, grads: step(
                span(index, number), keys_at(index, number), grads
            ),
            grads,
        )
        for p in range(pairs):
            pair = jnp.concatenate([grads[2 * p], grads[2 * p + 1]], axis=0).T * SCALE
            gp_ref[rows, lanes[p]] = turn(pair, cos_ref[place, :], -sin_ref[place, :]).astype(BF16)
        return carry

    lax.fori_loop(0, blocks, one_query, 0)

    def finish(code, carry):
        place = aligned(code)
        rows = aligned(inv_ref[code])
        for p in range(pairs):
            pair = dk_ref[place, lanes[p]] * SCALE
            at = slice(wide + p * LANES, wide + (p + 1) * LANES)
            gp_ref[rows, at] = turn(pair, cos_ref[place, :], -sin_ref[place, :]).astype(BF16)
            at = slice(2 * wide + p * LANES, 2 * wide + (p + 1) * LANES)
            gp_ref[rows, at] = dv_ref[place, lanes[p]].astype(BF16)
        return carry

    lax.fori_loop(0, blocks, finish, 0)


def attend_back(inv, query, key, value, grad, lse, cosine, sine, pairs, blocks):
    tokens = blocks * BLOCK
    wide = pairs * LANES
    vmem = pl.BlockSpec(memory_space=pltpu.VMEM)
    return pl.pallas_call(
        functools.partial(attend_back_kernel, pairs, blocks),
        out_shape=jax.ShapeDtypeStruct((tokens, 3 * wide), BF16),
        in_specs=[pl.BlockSpec(memory_space=pltpu.SMEM)] + [vmem] * 7,
        out_specs=vmem,
        scratch_shapes=[
            pltpu.VMEM((wide, tokens), BF16),
            pltpu.VMEM((tokens, wide), F32),
            pltpu.VMEM((tokens, wide), F32),
            pltpu.VMEM((2 * pairs, tokens, BLOCK), F32),
            pltpu.VMEM((2 * pairs, tokens, BLOCK), F32),
        ],
        compiler_params=pltpu.CompilerParams(vmem_limit_bytes=VMEM_MOST),
        cost_estimate=SHORT,
        name="attend_back",
    )(inv, query, key, value, grad, lse, cosine, sine)


def load_tile(pieces, out_ref, tile):
    start = 0
    for piece in pieces:
        cut = piece.shape[0]

        @pl.when(pl.program_id(0) == start // tile)
        def _(piece=piece, start=start % tile, cut=cut):
            out_ref[start : start + cut, :] = piece[...]

        start += cut


def whole(value):
    return pl.BlockSpec(value.shape, lambda i: (0, 0), pipeline_mode=pl.Buffered(1))


def norm_kernel(gain_ref, shift_ref, *refs):
    out_ref, held = refs[-2:]
    load_tile(refs[:-2], held, BLOCK)
    normed, _ = standardize(held[...].astype(F32))
    out_ref[...] = (normed * gain_ref[...] + shift_ref[...]).astype(BF16)


def norm_pieces(pieces, gain, shift):
    if not cube():
        return (standardize(pieces[0].astype(F32))[0] * gain + shift).astype(BF16)
    tokens = sum(piece.shape[0] for piece in pieces)
    values = (gain, shift, *pieces)
    return pl.pallas_call(
        norm_kernel,
        grid=(tokens // BLOCK,),
        out_shape=jax.ShapeDtypeStruct((tokens, D), BF16),
        in_specs=[whole(value) for value in values],
        out_specs=pl.BlockSpec((BLOCK, D), lambda i: (i, 0)),
        scratch_shapes=[pltpu.VMEM((BLOCK, D), BF16)],
        compiler_params=pltpu.CompilerParams(vmem_limit_bytes=VMEM_LIMIT),
        cost_estimate=SHORT,
        name="norm_pieces",
    )(*values)


def halves(value):
    half = value.shape[0] // 2
    return value[:half], value[half:]


def enter_feed(inputs, gain, shift, *parts):
    resid = inputs.astype(F32) + total_of(parts)
    normed, _ = standardize(resid)
    return (resid, *halves((normed * gain + shift).astype(BF16)))


def leave_feed(cotangent, resid, gain, *parts):
    grad = total_of(parts)
    normed, scaled = standardize(resid)
    grad_resid = cotangent.astype(F32) + norm_back(grad * gain, normed, scaled)
    sums = [jnp.sum(grad * normed, axis=0, keepdims=True), jnp.sum(grad, axis=0, keepdims=True)]
    return (grad_resid, *halves(grad_resid.astype(BF16)), *sums)


def leave_layer(inputs, grad_resid, gain, *parts):
    grad = total_of(parts)
    normed, scaled = standardize(inputs.astype(F32))
    sums = [jnp.sum(grad * normed, axis=0, keepdims=True), jnp.sum(grad, axis=0, keepdims=True)]
    return (grad_resid + norm_back(grad * gain, normed, scaled), *sums)


def own_kernel(step, count, *refs):
    results = step(*(ref[...] for ref in refs[:count]))
    for ref, result in zip(refs[count:], results):
        ref[...] = result


def own_rows(step, *values):
    if not cube():
        return step(*values)
    vmem = pl.BlockSpec(memory_space=pltpu.VMEM)
    shapes = jax.eval_shape(step, *values)
    return pl.pallas_call(
        functools.partial(own_kernel, step, len(values)),
        out_shape=shapes,
        in_specs=[vmem] * len(values),
        out_specs=tuple(vmem for _ in shapes),
        compiler_params=pltpu.CompilerParams(vmem_limit_bytes=VMEM_LIMIT),
        cost_estimate=SHORT,
        name=step.__name__,
    )(*values)


def ffn_up_kernel(units, count, w_ref, *refs):
    act_ref, both_ref, hidden_ref = refs[-3:]
    load_tile(refs[:count], act_ref, BLOCK)
    both_ref[...] = dot(act_ref[...], w_ref[...], 1, 0)
    gate = both_ref[:, :units]
    upper = both_ref[:, units:]
    hidden_ref[...] = (gate * jax.nn.sigmoid(gate) * upper).astype(BF16)


def ffn_up_step(pieces, weight, units, place, before):
    steps = sum(piece.shape[0] for piece in pieces) // BLOCK
    tokens = lax.axis_size("ctx") * BLOCK
    count = len(pieces)
    return pl.pallas_call(
        functools.partial(ffn_up_kernel, units, count),
        grid=(steps,),
        out_shape=(
            jax.ShapeDtypeStruct((tokens, D), BF16),
            jax.ShapeDtypeStruct((tokens, 2 * units), F32),
            jax.ShapeDtypeStruct((tokens, units), BF16),
        ),
        in_specs=[whole(weight)]
        + [whole(piece) for piece in pieces]
        + [pl.BlockSpec(memory_space=pl.ANY)] * len(before),
        out_specs=(
            pl.BlockSpec((BLOCK, D), lambda i: (place(i), 0)),
            pl.BlockSpec((BLOCK, 2 * units), lambda i: (place(i), 0)),
            pl.BlockSpec((BLOCK, units), lambda i: (place(i), 0)),
        ),
        input_output_aliases={1 + count + k: k for k in range(len(before))},
        compiler_params=pltpu.CompilerParams(vmem_limit_bytes=VMEM_LIMIT),
        cost_estimate=SHORT,
        name="ffn_up",
    )(weight, *pieces, *before)


def ffn_up(begun, weight, units):
    if not cube():
        act = begun[0]
        both = dot(act, weight, 1, 0)
        gate = both[:, :units]
        return act, both, (gate * jax.nn.sigmoid(gate) * both[:, units:]).astype(BF16)
    far = gather_far(begun)
    early = ffn_up_step(gather_near(begun), weight, units, lambda i: i + i // 3, ())
    far, early = tie(far, early)
    return ffn_up_step(gather_late(far), weight, units, lambda i: 3 + 4 * i, early)


def ffn_back_kernel(units, both_ref, cot_ref, down_ref, gb_ref):
    grad = dot(cot_ref[...], down_ref[...], 1, 1)
    gate = both_ref[:, :units]
    upper = both_ref[:, units:]
    sigma = jax.nn.sigmoid(gate)
    gb_ref[:, :units] = (grad * upper * sigma * (1.0 + gate * (1.0 - sigma))).astype(BF16)
    gb_ref[:, units:] = (grad * (gate * sigma)).astype(BF16)


def ffn_back(both, cot, down, units):
    if not cube():
        grad = dot(cot, down, 1, 1)
        gate = both[:, :units]
        sigma = jax.nn.sigmoid(gate)
        grad_gate = grad * both[:, units:] * sigma * (1.0 + gate * (1.0 - sigma))
        return jnp.concatenate([grad_gate, grad * (gate * sigma)], axis=1).astype(BF16)
    tokens = cot.shape[0]
    tile = 2 * BLOCK
    return pl.pallas_call(
        functools.partial(ffn_back_kernel, units),
        grid=(tokens // tile,),
        out_shape=jax.ShapeDtypeStruct((tokens, 2 * units), BF16),
        in_specs=[
            pl.BlockSpec((tile, 2 * units), lambda i: (i, 0)),
            pl.BlockSpec((tile, D), lambda i: (i, 0)),
            pl.BlockSpec((units, D), lambda i: (0, 0), pipeline_mode=pl.Buffered(1)),
        ],
        out_specs=pl.BlockSpec((tile, 2 * units), lambda i: (i, 0)),
        compiler_params=pltpu.CompilerParams(vmem_limit_bytes=VMEM_LIMIT),
        cost_estimate=SHORT,
        name="ffn_back",
    )(both, cot, down)


def branch_kernel(first, last, starts, mixed_ref, right_ref, *refs):
    count = len(starts)
    left_ref, grad_ref = refs[-2:]
    total = jnp.zeros(grad_ref.shape, F32)
    if not first:
        left_ref[...] = refs[count][...]
        total = refs[count + 1][...]
    for start, ref in zip(starts, refs):
        stop = start + ref.shape[0]
        left_ref[start:stop, :] = dot(ref[...], right_ref[...], 1, 1).astype(BF16)
        total += dot(mixed_ref[start:stop, :], ref[...], 0, 0)
    grad_ref[...] = total.astype(grad_ref.dtype)


def branch_step(mixed, right, pieces, starts, before, last):
    vmem = pl.BlockSpec(memory_space=pltpu.VMEM)
    values = (mixed, right, *pieces, *before)
    return pl.pallas_call(
        functools.partial(branch_kernel, not before, last, starts),
        out_shape=(
            jax.ShapeDtypeStruct(mixed.shape, BF16),
            jax.ShapeDtypeStruct((mixed.shape[1], D), BF16 if last else F32),
        ),
        in_specs=[vmem] * len(values),
        out_specs=(vmem, vmem),
        compiler_params=pltpu.CompilerParams(vmem_limit_bytes=VMEM_LIMIT),
        cost_estimate=SHORT,
        name="branch_step",
    )(*values)


def branch_grads(mixed, right, begun):
    if not cube():
        (whole_branch,) = begun
        left = dot(whole_branch, right, 1, 1).astype(BF16)
        return left, dot(mixed, whole_branch, 0, 0).astype(BF16)
    cut = BLOCK // 2
    places = tuple(range(6)) + tuple(range(8, 14)) + (6, 7, 14, 15)
    starts = tuple(place * cut for place in places)
    far = gather_far(begun)
    early = branch_step(mixed, right, gather_near(begun), starts[:12], (), False)
    far, early = tie(far, early)
    return branch_step(mixed, right, gather_late(far), starts[12:], early, True)


def turn_tables(blocks):
    prompt_blocks = blocks // 2
    later = CONT // BLOCK
    token = jnp.arange(blocks * BLOCK, dtype=jnp.int32)
    code = token // BLOCK
    inner = token % BLOCK
    place = jnp.where(
        code < prompt_blocks,
        token,
        prompt_blocks * BLOCK + (code - prompt_blocks) % later * BLOCK + inner,
    )
    half = ROTARY // 2
    freq = jnp.power(ROPE_BASE, -2.0 * jnp.arange(half, dtype=F32) / ROTARY)
    angle = place.astype(F32)[:, None] * freq[None, :]
    cosine, sine = jnp.cos(angle), jnp.sin(angle)
    rest = HEAD_DIM - ROTARY
    ones = jnp.ones((blocks * BLOCK, rest), F32)
    one_cos = jnp.concatenate([cosine, cosine, ones], axis=1)
    one_sin = jnp.concatenate([-sine, sine, 0.0 * ones], axis=1)
    return (jnp.tile(one_cos, (1, 2)), jnp.tile(one_sin, (1, 2)))


def local(
    layer_in,
    cotangent,
    block_map,
    attn_in,
    attn_out,
    ffn_in,
    ffn_out,
    vectors,
    first_attn_in,
    first_attn_out,
    first_ffn_in,
    first_ffn_out,
    first_vectors,
    second_attn_in,
    second_attn_out,
    second_ffn_in,
    second_ffn_out,
    second_vectors,
):
    cycle = lax.axis_size("ctx")
    groups = lax.axis_size("fsdp")
    here = lax.axis_index("ctx")
    owner = here * groups + lax.axis_index("fsdp")
    blocks = block_map.shape[1]
    rows = attn_in.shape[0]
    wide = D // cycle
    pairs = wide // LANES
    units = FF // cycle

    def rows_of(split):
        full = lax.all_gather(split, "fsdp", axis=0, tiled=False)
        return full.transpose(1, 0, 2, 3).reshape(D, split.shape[2])

    w_attn = lax.all_gather(attn_out.astype(BF16), "fsdp", axis=0, tiled=True)
    mine = vectors.astype(BF16).T.reshape(1, 7 * rows)
    below = jnp.pad(mine, ((0, 15), (0, 3 * wide - 7 * rows)))
    qkv_split = exchange(split_columns(attn_in, 3, below))
    w_qkv = rows_of(qkv_split[:, :rows])

    vec = qkv_split[:, rows, : 7 * rows].reshape(1, cycle, 7, rows)
    vec = lax.dynamic_update_slice(
        jnp.zeros((groups, cycle, 7, rows), BF16), vec, (lax.axis_index("fsdp"), 0, 0, 0)
    )
    vec = sum_everywhere(vec, ("fsdp",)).transpose(2, 1, 0, 3).reshape(7, D).astype(F32)

    inv = jnp.argsort(block_map[0][places()]).astype(jnp.int32)
    x_pieces, vec, w_attn, ffn_in_late, cot_own, inv, cosine, sine = tie(
        gather_pieces(gather_start(*halves(layer_in[0]))),
        vec,
        w_attn,
        ffn_in,
        cotangent[0],
        inv,
        *turn_tables(blocks),
    )
    attn_act = norm_pieces(x_pieces, vec[0:1], vec[1:2])
    up_split, down_own, attn_act = tie(
        exchange(split_columns(ffn_in_late, 2)), ffn_out.astype(BF16), attn_act
    )
    w_up = rows_of(up_split)
    w_down = lax.all_gather(down_own, "fsdp", axis=0, tiled=True)

    bias = lax.dynamic_slice_in_dim(vec[2:5], here * wide, wide, 1).reshape(1, 3 * wide)
    project = dot(attn_act, w_qkv, 1, 0)
    project, cot_begun = tie(project, gather_start(*halves(cot_own)))
    query, key, value, mixed, lse = attend(inv, project, bias, cosine, sine, pairs, blocks)
    cot_far = gather_far(cot_begun)
    mixed, cot_far = tie(mixed, cot_far)
    away = scatter_away(mixed, w_attn, 0)
    begun = scatter_start(scatter_sums(mixed, w_attn, 0, away))
    cot_low = jnp.concatenate(gather_pieces(cot_begun, cot_far), axis=0)
    begun, cot_low, w_up = window(begun, cot_low, w_up)
    parts = scatter_end(begun)
    resid, act_top, act_low = own_rows(enter_feed, layer_in[0], vec[5:6], vec[6:7], *parts)

    def owners(grad):
        return lax.psum_scatter(grad, "fsdp", scatter_dimension=0, tiled=True)

    def by_owner(grad):
        wider = grad.shape[1]
        return grad.reshape(-1, groups, rows, wider).transpose(1, 0, 2, 3).reshape(-1, wider)

    def owners_of_rows(grad):
        return owners(grad).reshape(-1, rows, grad.shape[1])

    ffn_act, both, hidden = ffn_up(gather_start(act_top, act_low), w_up, units)
    grad_both = ffn_back(both, cot_low, w_down, units)
    away = scatter_away(grad_both, w_up, 1)
    away, grad_down = tie(away, dot(hidden, cot_low, 0, 0).astype(BF16))
    share_down = owners(grad_down)
    begun = scatter_start(scatter_sums(grad_both, w_up, 1, away))
    grad_in = by_owner(dot(ffn_act, grad_both, 0, 0).astype(BF16))
    parts, grad_in = tie(scatter_end(begun), grad_in)
    share_in = owners_of_rows(grad_in)
    grad_resid, branch_top, branch_low, gain_two, shift_two = own_rows(
        leave_feed, cotangent[0], resid, vec[5:6], *parts
    )

    begun = gather_start(branch_top, branch_low, True)
    if cube():
        c_top, hidden = tie(begun[2], hidden)
        begun = (*begun[:2], c_top, *begun[3:])
    out_sums = scatter_sums(hidden, w_down, 0, scatter_away(hidden, w_down, 0))
    begun, out_sums = window(begun, out_sums)
    grad_mixed, grad_out = branch_grads(mixed, w_attn, begun)
    grad_mixed, out_sums, share_down = tie(grad_mixed, out_sums, share_down)
    out_begun = scatter_start(out_sums, False)
    grad_project = attend_back(
        inv, query, key, value, grad_mixed, lse, cosine, sine, pairs, blocks
    )
    grad_project, out_begun, share_in = tie(grad_project, out_begun, share_in)
    out_parts = scatter_end(out_begun)
    away = scatter_away(grad_project, w_qkv, 1)
    grad_qkv = by_owner(dot(attn_act, grad_project, 0, 0).astype(BF16))
    away, grad_qkv = tie(away, grad_qkv)
    share_qkv = owners_of_rows(grad_qkv)
    sums = scatter_sums(grad_project, w_qkv, 1, away)
    sums, grad_project, out_parts, share_in, grad_out, share_down = tie(
        sums, grad_project, out_parts, share_in, grad_out, share_down
    )
    place = lax.axis_index("fsdp")
    share_out = F32(0.0)
    for m in range(groups):
        block = lax.dynamic_slice_in_dim(grad_out, (place ^ m) * rows, rows, 0)
        share_out = share_out + (swap(block, m, "fsdp") if m else block).astype(F32)
    layer_out = (resid + total_of(out_parts)).astype(BF16)[None]
    bias_grads = jnp.sum(grad_project.astype(F32), axis=0).reshape(3, wide)
    bias_grads = lax.dynamic_update_slice(jnp.zeros((3, D), F32), bias_grads, (0, here * wide))
    squares = squared(share_in) + squared(share_out) + squared(share_down)
    parts, layer_out, bias_grads, squares, share_in = tie(
        scatter_end(scatter_start(sums)), layer_out, bias_grads, squares, share_in
    )
    split_in = exchange(share_in)
    input_grad, gain_one, shift_one = own_rows(
        leave_layer, layer_in[0], grad_resid, vec[0:1], *parts
    )
    gain_one, shift_one, share_qkv = tie(gain_one, shift_one, share_qkv)
    split_qkv = exchange(share_qkv)

    squares = squares + squared(share_qkv)
    sums = jnp.concatenate(
        [
            gain_one,
            shift_one,
            bias_grads,
            gain_two,
            shift_two,
            jnp.where(jnp.arange(D)[None] == 0, squares, 0.0),
        ],
        axis=0,
    )
    sums = sum_everywhere(sums)
    vector_sums = sums[:7]
    grad_norm = jnp.sqrt(jnp.sum(vector_sums * vector_sums) + sums[7, 0])
    mine = jnp.arange(D)[:, None] == owner * rows + jnp.arange(rows)[None]
    vector_grads = lax.dot_general(
        mine.astype(F32), vector_sums, (((0,), (1,)), ((), ())), precision=lax.Precision.HIGHEST
    )
    clip = jnp.minimum(1.0, CLIP_LIMIT / (grad_norm + 1e-06))
    grad_list = (
        join_columns(split_qkv, 3),
        share_out,
        join_columns(split_in, 2),
        share_down,
        vector_grads,
    )
    rates = (D ** (-0.5), 0.6 * max(D // 64, 32) ** (-0.5), D ** (-0.5), (FF // 4) ** (-0.5), 0.3)
    weights = (attn_in, attn_out, ffn_in, ffn_out, vectors)
    firsts = (first_attn_in, first_attn_out, first_ffn_in, first_ffn_out, first_vectors)
    seconds = (second_attn_in, second_attn_out, second_ffn_in, second_ffn_out, second_vectors)
    updated = []
    for index in range(5):
        updated.extend(
            adam(
                weights[index], clip * grad_list[index].astype(F32), firsts[index], seconds[index], rates[index]
            )
        )
    return (layer_out, input_grad[None], grad_norm, *updated)


def solution(mesh):
    tokens = P("fsdp", "ctx", None)
    owned = P(("ctx", "fsdp"), None)
    return jax.shard_map(
        local,
        mesh=mesh,
        in_specs=(tokens, tokens, P("fsdp", None)) + (owned,) * 15,
        out_specs=(tokens, tokens, P()) + (owned,) * 15,
        check_vma=False,
    )
```
